256 devices in a mesh: seq: 16 (over z, x_lo), head: 16 (over x_hi, y, core).
Axes of the slice: x: 4 (x_hi: 2, x_lo: 2; x = x_hi * 2 + x_lo), y: 4, z: 8, core: 2. Of those that a mesh axis runs over, the one named last changes fastest.
Arguments:
- teacher: bfloat16 [3, 4096, 8192], P(None, 'seq', 'head'), may hold values from -10 to 10
- student: bfloat16 [3, 4096, 4096], P(None, 'seq', 'head'), may hold values from -10 to 10
- weights: float32 [4096], P('seq'), may hold values from 64 to 512
- lengths: int32 [4], replicated, may hold values from 1 to 3072, 4096 in all
Outputs:
- row_loss: float32 [4096], P('seq')
- student_grad: float32 [3, 4096, 4096], P(None, 'seq', 'head')
The draws below stay inside these ranges and needn't reach their ends.
Inputs may be any that keep to these rules, and one draw needn't show every extreme that they name: The lengths sum to 4096; the longest document has exactly 3072 tokens.
All inputs are finite; a program needn't handle non-finite values.
Results may differ from the reference program's by a relative error of at most 0.0044.
Values may be sent and summed in bfloat16 or wider, within the bound.
No kernel may reach another device: no remote copies, remote signals or barrier semaphores. Data moves between devices by JAX's collectives and lax.ppermute only.
A program may use at most 128 MiB of HBM per device.

```python
import math
import jax
import jax.numpy as jnp
import numpy as np
from jax import lax

DT = 512
DS = 256
RELS = 3
DOCS = 4
HEADS = 16
TOKENS = 4096


def draw_teacher(key, part):
    key = jax.random.fold_in(key, 11)
    base_key = jax.random.fold_in(key, 0)
    return jnp.clip(0.6 * jax.random.normal(base_key, (RELS, TOKENS, HEADS * DT), jnp.float32), -3.0, 3.0).astype(jnp.bfloat16)


def draw_student(key, part):
    key = jax.random.fold_in(key, 23)
    base_key = jax.random.fold_in(key, 0)
    return jnp.clip(0.6 * jax.random.normal(base_key, (RELS, TOKENS, HEADS * DS), jnp.float32), -3.0, 3.0).astype(jnp.bfloat16)


def shard_levels(rng, extent, shards, smallest, top_value):
    def one(dim, shards_of):
        heights = jax.random.uniform(jax.random.fold_in(jax.random.fold_in(rng, 6), dim), (shards_of,), jnp.float32, smallest / len(shards), top_value / len(shards))
        return jnp.repeat(jnp.exp(heights), extent[dim] // shards_of).reshape((-1,) + (1,) * (len(extent) - dim - 1))

    loudness = one(*shards[0])
    for cut in shards[1:]:
        loudness = loudness * one(*cut)
    return loudness


def length_profile(amount, total, bound, skew):
    portions = [(1 << 20) // math.isqrt(grade ** skew) + 1 for grade in range(2, amount + 1)]
    rest, counts = total - bound - (amount - 1), [1] * (amount - 1)
    while rest > 0:
        free = [i for i in range(amount - 1) if counts[i] < bound]
        pool, left = sum([portions[i] for i in free]), rest
        for i in free:
            addition = min(bound - counts[i], max(1, left * portions[i] // pool), rest)
            counts[i] = counts[i] + addition
            rest = rest - addition
    return np.array([bound] + counts)


def uneven(key, count, total, most, slope):
    if count == 2:
        one = jax.random.randint(key, (), max(1, total - most), min(most, total - 1) + 1)
        return jnp.stack([one, total - one])
    sizes = jnp.asarray(length_profile(count, total, most, slope), jnp.int32)
    twos = (count - 1) // 2
    giver, receiver = sizes[1:1 + 2 * twos:2], sizes[2:2 + 2 * twos:2]
    margin = jnp.minimum(giver - 1, most - receiver)
    passed = jax.random.randint(jax.random.fold_in(key, 1), (twos,), 0, 1 << 20) % (margin + 1)
    sizes = sizes.at[1:1 + 2 * twos:2].set(giver - passed).at[2:2 + 2 * twos:2].set(receiver + passed)
    return sizes[jax.random.permutation(jax.random.fold_in(key, 2), count)]


def setup_inputs(seed: int = 0) -> dict:
    keys = jax.random.split(jax.random.key(seed), 5)
    return {
        "teacher": draw_teacher(jax.random.fold_in(keys[4], 71), 0),
        "student": draw_student(jax.random.fold_in(keys[4], 71), 0),
        "weights": jnp.clip(jnp.exp(math.log(512.0) - 2.0794415 * jax.random.uniform(keys[2], (TOKENS,), jnp.float32) ** shard_levels(keys[2], (TOKENS,), ((0, 16),), -0.2, 0.2)), 64.0, 512.0),
        "lengths": uneven(keys[3], DOCS, TOKENS, 3 * TOKENS // 4, 0).astype(jnp.int32),
    }


NEG_FILL = -1e+30

def reference(teacher, student, weights, lengths):
    doc_ends = jnp.cumsum(lengths)
    positions = jnp.arange(TOKENS, dtype=jnp.int32)
    docs = lax.optimization_barrier(jnp.sum((positions[:, None] >= doc_ends[None, :]).astype(jnp.int32), axis=1))
    keep = docs[:, None] == docs[None, :]
    teacher_scale = 1.0 / math.sqrt(DT)
    student_scale = 1.0 / math.sqrt(DS)

    def normalizer(scores):
        top = lax.optimization_barrier(jnp.max(jnp.where(keep, scores, NEG_FILL), axis=1))
        total = lax.optimization_barrier(jnp.sum(jnp.where(keep, jnp.exp(scores - top[:, None]), 0.0), axis=1))
        return top + jnp.log(total)

    def one_head(item):
        relation = item // HEADS
        head_index = item % HEADS
        teacher_anchor = (relation, jnp.int32(0), (head_index * DT).astype(jnp.int32))
        student_anchor = (relation, jnp.int32(0), (head_index * DS).astype(jnp.int32))
        teacher_rows = lax.dynamic_slice(teacher, teacher_anchor, (1, TOKENS, DT))[0]
        student_rows = lax.dynamic_slice(student, student_anchor, (1, TOKENS, DS))[0]
        teacher_scores = teacher_scale * jnp.dot(teacher_rows, teacher_rows.T, preferred_element_type=jnp.float32)
        student_scores = student_scale * jnp.dot(student_rows, student_rows.T, preferred_element_type=jnp.float32)
        teacher_lse = normalizer(teacher_scores)
        student_lse = normalizer(student_scores)
        teacher_probs = jnp.exp(jnp.where(keep, teacher_scores - teacher_lse[:, None], NEG_FILL))
        student_probs = jnp.exp(jnp.where(keep, student_scores - student_lse[:, None], NEG_FILL))
        divergence = lax.optimization_barrier(jnp.sum(teacher_probs * (teacher_scores - student_scores), axis=1)) - teacher_lse + student_lse
        pull = weights[:, None] * (student_probs - teacher_probs)
        symmetric = (pull + pull.T).astype(jnp.bfloat16)
        grad_rows = student_scale * jnp.dot(symmetric, student_rows, preferred_element_type=jnp.float32)
        return (divergence, grad_rows)
    items = jnp.arange(RELS * HEADS, dtype=jnp.int32)
    divergence, grads = lax.map(one_head, items)
    row_loss = lax.optimization_barrier(jnp.sum(divergence, axis=0))
    student_grad = grads.reshape(RELS, HEADS, TOKENS, DS).transpose(0, 2, 1, 3).reshape(RELS, TOKENS, HEADS * DS)
    return (row_loss, student_grad)
```

```python
import functools
import math

import jax
import jax.numpy as jnp
from jax import lax
from jax.experimental import pallas as pl
from jax.experimental.pallas import tpu as pltpu
from jax.sharding import PartitionSpec as P

AXES = ("seq", "head")
PLANES = (0, 1, 2, 4, 5, 6)
BLOCK = 256
WIDE = 512
NARROW = 256
LOG2E = math.log2(math.e)
LN2 = math.log(2.0)
TEACHER_SCALE = 1.0 / math.sqrt(WIDE)
STUDENT_SCALE = 1.0 / math.sqrt(NARROW)
NEG_FILL = -1e30
SUM_LIMIT = 1e30
LSE_LIMIT = 60.0
MIB = 1 << 20


def place(z, x, g, c):
    return (z * 2 + x) * 16 + g * 2 + c


DEVICES = [(z, x, g, c) for z in range(8) for x in range(2) for g in range(8) for c in range(2)]


def out_pairs(k):
    pairs = []
    for z, x, g, c in DEVICES:
        r = (z // 2 - k) % 4
        if r < 3:
            pairs.append((place(z, x, g, c), place(PLANES[c * 3 + r], x, g, z % 2)))
    return pairs


def back_pairs(k):
    return [(b, a) for a, b in out_pairs(k)]


def swap_pairs(dx, dc):
    return [(place(z, x, g, c), place(z, x ^ dx, g, c ^ dc)) for z, x, g, c in DEVICES if z in PLANES]


def permute(value, pairs):
    return lax.ppermute(value, AXES, pairs)


NT = (((1,), (1,)), ((), ()))
NN = (((1,), (0,)), ((), ()))


def dot(a, b, dims):
    return lax.dot_general(a, b, dims, preferred_element_type=jnp.float32)


def scores(rows, keys):
    t = dot(rows[:, :WIDE], keys[:, :WIDE], NT) * (TEACHER_SCALE * LOG2E)
    s = dot(rows[:, WIDE:], keys[:, WIDE:], NT) * (STUDENT_SCALE * LOG2E)
    return t, s


def doc_of(positions, ends_ref):
    total = jnp.zeros(positions.shape, jnp.int32)
    for d in range(4):
        total += jnp.where(positions >= ends_ref[d], 1, 0)
    return total


def keep_mask(row_base, key_base, ends_ref):
    rows = row_base + lax.broadcasted_iota(jnp.int32, (BLOCK, 1), 0)
    keys = key_base + lax.broadcasted_iota(jnp.int32, (1, BLOCK), 1)
    return doc_of(rows, ends_ref) == doc_of(keys, ends_ref)


def relation_of(r, k, spans_ref):
    touch = jnp.logical_and(spans_ref[1, r] <= spans_ref[2, k], spans_ref[1, k] <= spans_ref[2, r])
    whole = jnp.logical_and(
        jnp.logical_and(spans_ref[1, r] == spans_ref[2, r], spans_ref[1, k] == spans_ref[2, k]),
        spans_ref[1, r] == spans_ref[1, k],
    )
    return touch, whole


def lane_sum(v):
    return v[:, :128] + v[:, 128:]


def as_row(v):
    return jnp.sum(v.T, axis=0, keepdims=True)


def as_column(row):
    return jnp.broadcast_to(row, (128, BLOCK)).T


def both_halves(v):
    return jnp.concatenate([v, v], axis=1)


def stats_kernel(spans_ref, ends_ref, w_ref, *refs):
    keys = refs[:16]
    out_ref, own, spare, acc_t, acc_c, acc_s, max_t, max_s = refs[16:]
    for k in range(4):
        own[k] = keys[4 * k][...]
    out_ref[...] = jnp.zeros_like(out_ref)

    @pl.loop(0, 4)
    def _(rb):
        acc_t[...] = jnp.zeros_like(acc_t)
        acc_c[...] = jnp.zeros_like(acc_c)
        acc_s[...] = jnp.zeros_like(acc_s)
        slot = 4 * rb

        def tile(kb, masked):
            t, s = scores(own[rb], keys[kb][...])
            et = jnp.exp2(t)
            es = jnp.exp2(s)
            if masked:
                keep = keep_mask(spans_ref[0, slot], spans_ref[0, kb], ends_ref)
                et = jnp.where(keep, et, 0.0)
                es = jnp.where(keep, es, 0.0)
            acc_t[...] += lane_sum(et)
            acc_s[...] += lane_sum(es)
            acc_c[...] += lane_sum(et * (t - s))

        for kb in range(16):
            touch, whole = relation_of(slot, kb, spans_ref)
            pl.when(jnp.logical_and(touch, whole))(functools.partial(tile, kb, False))
            pl.when(jnp.logical_and(touch, jnp.logical_not(whole)))(functools.partial(tile, kb, True))

        sum_t = as_row(acc_t[...])
        sum_s = as_row(acc_s[...])
        lse_t = jnp.log(sum_t)
        lse_s = jnp.log(sum_s)
        out_ref[rb, 0:1] = lse_t
        out_ref[rb, 1:2] = lse_s
        out_ref[rb, 2:3] = as_row(acc_c[...]) * LN2 / sum_t - lse_t + lse_s
        out_ref[rb, 3:4] = w_ref[rb]
        fine = jnp.logical_and(jnp.max(sum_t) < SUM_LIMIT, jnp.max(sum_s) < SUM_LIMIT)

        @pl.when(jnp.logical_not(fine))
        def _():
            acc_t[...] = jnp.zeros_like(acc_t)
            acc_c[...] = jnp.zeros_like(acc_c)
            acc_s[...] = jnp.zeros_like(acc_s)
            max_t[...] = jnp.full_like(max_t, NEG_FILL)
            max_s[...] = jnp.full_like(max_s, NEG_FILL)

            @pl.loop(0, 16)
            def _(kb):
                for i in range(16):

                    @pl.when(kb == i)
                    def _():
                        spare[...] = keys[i][...]

                touch, _w = relation_of(slot, kb, spans_ref)

                @pl.when(touch)
                def _():
                    t, s = scores(own[rb], spare[...])
                    keep = keep_mask(spans_ref[0, slot], spans_ref[0, kb], ends_ref)
                    kept_t = jnp.where(keep, t, NEG_FILL)
                    kept_s = jnp.where(keep, s, NEG_FILL)
                    old_t = max_t[...]
                    old_s = max_s[...]
                    new_t = jnp.maximum(old_t, jnp.max(kept_t, axis=1, keepdims=True))
                    new_s = jnp.maximum(old_s, jnp.max(kept_s, axis=1, keepdims=True))
                    et = jnp.where(keep, jnp.exp2(kept_t - new_t[:, :1]), 0.0)
                    es = jnp.where(keep, jnp.exp2(kept_s - new_s[:, :1]), 0.0)
                    shrink_t = jnp.exp2(old_t - new_t)
                    acc_t[...] = acc_t[...] * shrink_t + lane_sum(et)
                    acc_c[...] = acc_c[...] * shrink_t + lane_sum(et * (t - s))
                    acc_s[...] = acc_s[...] * jnp.exp2(old_s - new_s) + lane_sum(es)
                    max_t[...] = new_t
                    max_s[...] = new_s

            sum_t = as_row(acc_t[...])
            sum_s = as_row(acc_s[...])
            lse_t = jnp.log(sum_t) + LN2 * max_t[...].T[0:1]
            lse_s = jnp.log(sum_s) + LN2 * max_s[...].T[0:1]
            out_ref[rb, 0:1] = lse_t
            out_ref[rb, 1:2] = lse_s
            out_ref[rb, 2:3] = as_row(acc_c[...]) * LN2 / sum_t - lse_t + lse_s


def grad_kernel(spans_ref, ends_ref, *refs):
    stats = refs[:4]
    keys = refs[4:20]
    out_ref, own, spare, key_u, row_u, acc = refs[20:]
    for k in range(4):
        own[k] = keys[4 * k][...]
    top = stats[0][0, 0:2]
    for k in range(4):
        for i in range(4):
            lse = stats[i][k, 0:2]
            top = jnp.maximum(top, lse)
            key_u[4 * k + i, 0:2] = stats[i][k, 3:4] * jnp.exp(-lse)
            key_u[4 * k + i, 2:4] = lse * LOG2E
            key_u[4 * k + i, 4:5] = stats[i][k, 3:4]
    calm = jnp.max(top) <= LSE_LIMIT

    @pl.loop(0, 4)
    def _(rb):
        acc[...] = jnp.zeros_like(acc)
        slot = 4 * rb
        for i in range(5):
            row_u[i] = as_column(key_u[slot, i : i + 1])

        def tile(kb, masked):
            t, s = scores(own[rb], keys[kb][...])
            row_t = both_halves(row_u[0])
            row_s = both_halves(row_u[1])
            symmetric = jnp.exp2(s) * (row_s + key_u[kb, 1:2]) - jnp.exp2(t) * (row_t + key_u[kb, 0:1])
            if masked:
                keep = keep_mask(spans_ref[0, slot], spans_ref[0, kb], ends_ref)
                symmetric = jnp.where(keep, symmetric, 0.0)
            acc[...] += dot(symmetric.astype(jnp.bfloat16), keys[kb][:, WIDE:], NN)

        @pl.when(calm)
        def _():
            for kb in range(16):
                touch, whole = relation_of(slot, kb, spans_ref)
                pl.when(jnp.logical_and(touch, whole))(functools.partial(tile, kb, False))
                pl.when(jnp.logical_and(touch, jnp.logical_not(whole)))(functools.partial(tile, kb, True))

        @pl.when(jnp.logical_not(calm))
        def _():
            @pl.loop(0, 16)
            def _(kb):
                for i in range(16):

                    @pl.when(kb == i)
                    def _():
                        spare[...] = keys[i][...]

                touch, _w = relation_of(slot, kb, spans_ref)

                @pl.when(touch)
                def _():
                    t, s = scores(own[rb], spare[...])
                    keep = keep_mask(spans_ref[0, slot], spans_ref[0, kb], ends_ref)
                    key = key_u[kb]

                    def prob(score, lse):
                        return jnp.exp2(jnp.where(keep, score - lse, NEG_FILL))

                    pull = both_halves(row_u[4]) * (
                        prob(s, both_halves(row_u[3])) - prob(t, both_halves(row_u[2]))
                    )
                    pull_t = key[4:5] * (prob(s, key[3:4]) - prob(t, key[2:3]))
                    symmetric = (pull + pull_t).astype(jnp.bfloat16)
                    acc[...] += dot(symmetric, spare[:, WIDE:], NN)

        out_ref[rb] = (acc[...] * STUDENT_SCALE).astype(out_ref.dtype)


VMEM = pl.BlockSpec(memory_space=pltpu.VMEM)
SMEM = pl.BlockSpec(memory_space=pltpu.SMEM)


def run_stats(spans, ends, w, keys):
    return pl.pallas_call(
        stats_kernel,
        out_shape=jax.ShapeDtypeStruct((4, 8, BLOCK), jnp.float32),
        in_specs=[SMEM, SMEM, VMEM] + [VMEM] * 16,
        out_specs=VMEM,
        scratch_shapes=[
            pltpu.VMEM((4, BLOCK, WIDE + NARROW), jnp.bfloat16),
            pltpu.VMEM((BLOCK, WIDE + NARROW), jnp.bfloat16),
        ]
        + [pltpu.VMEM((BLOCK, 128), jnp.float32)] * 5,
        compiler_params=pltpu.CompilerParams(vmem_limit_bytes=32 * MIB),
        name="stats",
    )(spans, ends, w, *keys)


def run_grad(spans, ends, stats, keys):
    return pl.pallas_call(
        grad_kernel,
        out_shape=jax.ShapeDtypeStruct((4, BLOCK, NARROW), jnp.bfloat16),
        in_specs=[SMEM, SMEM] + [VMEM] * 20,
        out_specs=VMEM,
        scratch_shapes=[
            pltpu.VMEM((4, BLOCK, WIDE + NARROW), jnp.bfloat16),
            pltpu.VMEM((BLOCK, WIDE + NARROW), jnp.bfloat16),
            pltpu.VMEM((16, 8, BLOCK), jnp.float32),
            pltpu.VMEM((5, BLOCK, 128), jnp.float32),
            pltpu.VMEM((BLOCK, NARROW), jnp.float32),
        ],
        compiler_params=pltpu.CompilerParams(vmem_limit_bytes=32 * MIB),
        name="grad",
    )(spans, ends, *stats, *keys)


def local(teacher, student, weights, lengths):
    seq = lax.axis_index("seq")
    z, x = seq // 2, seq % 2
    c = lax.axis_index("head") % 2
    quad = z // 2

    relation = jnp.int32(0)
    for index, plane in enumerate(PLANES):
        relation = jnp.where(z == plane, index % 3, relation)

    own, w_rows = [], []
    w_out = weights.reshape(1, BLOCK)
    for k in range(4):
        r = jnp.minimum((quad - k) % 4, 2)
        block = jnp.concatenate(
            [
                lax.dynamic_index_in_dim(teacher, r, 0, False),
                lax.dynamic_index_in_dim(student, r, 0, False),
            ],
            axis=1,
        )
        own.append(permute(block, out_pairs(k)))
    core = [permute(v, swap_pairs(0, 1)) for v in own]
    side = [permute(v, swap_pairs(1, 0)) for v in own]
    side_core = [permute(v, swap_pairs(0, 1)) for v in side]
    for k in range(4):
        w_rows.append(permute(w_out, out_pairs(k)))
    keys = [v[k] for k in range(4) for v in (own, core, side, side_core)]

    ends = jnp.cumsum(lengths)
    mine = 2 * c + x
    base = []
    for k in range(4):
        for flip in (0, 2, 1, 3):
            base.append((((k + relation) % 4) * 4 + (mine ^ flip)) * BLOCK)
    base = jnp.stack(base).astype(jnp.int32)

    def doc(positions):
        return jnp.sum((positions[:, None] >= ends[None, :]).astype(jnp.int32), axis=1)

    spans = jnp.stack([base, doc(base), doc(base + (BLOCK - 1))])

    stats = run_stats(spans, ends, jnp.stack(w_rows), keys)
    all_stats = [stats] + [permute(stats, swap_pairs(dx, dc)) for dx, dc in ((0, 1), (1, 0), (1, 1))]
    grads = run_grad(spans, ends, all_stats, keys)

    total = sum(permute(stats[k, 2:3], back_pairs(k)) for k in range(4))
    for flip in (1, 2, 4, 8):
        total = total + permute(
            total, [(place(z, x, g, c), place(z, x, g, c) ^ flip) for z, x, g, c in DEVICES]
        )
    row_loss = total.reshape(BLOCK)

    back = jnp.stack([permute(grads[k], back_pairs(k)) for k in range(4)])
    student_grad = jnp.stack(
        [lax.dynamic_index_in_dim(back, (quad - r) % 4, 0, False) for r in range(3)]
    ).astype(jnp.float32)
    return (row_loss, student_grad)


def solution(mesh):
    return jax.shard_map(
        local,
        mesh=mesh,
        in_specs=(P(None, "seq", "head"), P(None, "seq", "head"), P("seq"), P()),
        out_specs=(P("seq"), P(None, "seq", "head")),
        check_vma=False,
    )
```

```python
import functools
import math

import jax
import jax.numpy as jnp
from jax import lax
from jax.experimental import pallas as pl
from jax.experimental.pallas import tpu as pltpu
from jax.sharding import PartitionSpec as P

AXES = ("seq", "head")
PLANES = (0, 1, 2, 4, 5, 6)
BLOCK = 256
WIDE = 512
NARROW = 256
LOG2E = math.log2(math.e)
LN2 = math.log(2.0)
TEACHER_SCALE = 1.0 / math.sqrt(WIDE)
STUDENT_SCALE = 1.0 / math.sqrt(NARROW)
NEG_FILL = -1e30
SUM_LIMIT = 1e30
LSE_LIMIT = 60.0
MIB = 1 << 20


def place(z, x, g, c):
    return (z * 2 + x) * 16 + g * 2 + c


DEVICES = [(z, x, g, c) for z in range(8) for x in range(2) for g in range(8) for c in range(2)]


def out_pairs(k):
    pairs = []
    for z, x, g, c in DEVICES:
        r = (z // 2 - k) % 4
        if r < 3:
            pairs.append((place(z, x, g, c), place(PLANES[c * 3 + r], x, g, z % 2)))
    return pairs


def back_pairs(k):
    return [(b, a) for a, b in out_pairs(k)]


def swap_pairs(dx, dc):
    return [(place(z, x, g, c), place(z, x ^ dx, g, c ^ dc)) for z, x, g, c in DEVICES if z in PLANES]


def permute(value, pairs):
    return lax.ppermute(value, AXES, pairs)


NT = (((1,), (1,)), ((), ()))
NN = (((1,), (0,)), ((), ()))


def dot(a, b, dims):
    return lax.dot_general(a, b, dims, preferred_element_type=jnp.float32)


def scores(rows, keys):
    t = dot(rows[:, :WIDE], keys[:, :WIDE], NT) * (TEACHER_SCALE * LOG2E)
    s = dot(rows[:, WIDE:], keys[:, WIDE:], NT) * (STUDENT_SCALE * LOG2E)
    return t, s


def doc_of(positions, ends_ref):
    total = jnp.zeros(positions.shape, jnp.int32)
    for d in range(4):
        total += jnp.where(positions >= ends_ref[d], 1, 0)
    return total


def down(base):
    return base + lax.broadcasted_iota(jnp.int32, (BLOCK, 1), 0)


def across(base):
    return base + lax.broadcasted_iota(jnp.int32, (1, BLOCK), 1)


def within(positions, plan_ref):
    return jnp.logical_and(positions >= plan_ref[6, 0], positions < plan_ref[6, 1])


def fold(v):
    return jnp.sum(v.reshape(BLOCK // 8, 8, BLOCK), axis=0)


def as_row(v):
    return jnp.sum(v, axis=0, keepdims=True)


def as_column(row):
    return jnp.broadcast_to(row, (128, BLOCK)).T


def both_halves(v):
    return jnp.concatenate([v, v], axis=1)


def block_at(ref, index):
    return ref.at[pl.ds(pl.multiple_of(index * BLOCK, BLOCK), BLOCK)]


LONG_TILES = 13
SHORT_TILES = 5


def stats_kernel(plan_ref, ends_ref, w_ref, keys_ref, out_ref, sums, max_t, max_s):
    out_ref[...] = jnp.zeros_like(out_ref)

    @pl.loop(0, 4)
    def _(rb):
        own_block = plan_ref[0, rb]
        own = block_at(keys_ref, own_block)
        row_positions = across(own_block * BLOCK)
        sums[...] = jnp.zeros_like(sums)

        def gather_tiles(first, count, keep_of):
            part_t = jnp.zeros((8, BLOCK), jnp.float32)
            part_c = jnp.zeros((8, BLOCK), jnp.float32)
            part_s = jnp.zeros((8, BLOCK), jnp.float32)
            for j in range(count):
                t, s = scores(block_at(keys_ref, first + j)[...], own[...])
                et = jnp.exp2(t)
                es = jnp.exp2(s)
                keep = keep_of(j)
                if keep is not None:
                    et = jnp.where(keep, et, 0.0)
                    es = jnp.where(keep, es, 0.0)
                part_t += fold(et)
                part_s += fold(es)
                part_c += fold(et * (t - s))
            return as_row(part_t), as_row(part_s), as_row(part_c)

        @pl.when(plan_ref[1, rb] == 1)
        def _():
            first = plan_ref[6, 2]

            def keep_of(j):
                if 0 < j < LONG_TILES - 1:
                    return None
                return within(down((first + j) * BLOCK), plan_ref)

            st, ss, sc = gather_tiles(first, LONG_TILES, keep_of)
            mine = within(row_positions, plan_ref)
            sums[0:1] = jnp.where(mine, st, 0.0)
            sums[1:2] = jnp.where(mine, ss, 0.0)
            sums[2:3] = jnp.where(mine, sc, 0.0)

        @pl.when(plan_ref[3, rb] > 0)
        def _():
            first = plan_ref[2, rb]
            row_docs = doc_of(row_positions, ends_ref)

            def keep_of(j):
                return doc_of(down((first + j) * BLOCK), ends_ref) == row_docs

            st, ss, sc = gather_tiles(first, SHORT_TILES, keep_of)
            mine = within(row_positions, plan_ref)
            sums[0:1] = jnp.where(mine, sums[0:1], st)
            sums[1:2] = jnp.where(mine, sums[1:2], ss)
            sums[2:3] = jnp.where(mine, sums[2:3], sc)

        fine = jnp.logical_and(jnp.max(sums[0:1]) < SUM_LIMIT, jnp.max(sums[1:2]) < SUM_LIMIT)

        @pl.when(jnp.logical_not(fine))
        def _():
            sums[...] = jnp.zeros_like(sums)
            max_t[...] = jnp.full_like(max_t, NEG_FILL)
            max_s[...] = jnp.full_like(max_s, NEG_FILL)
            row_docs = doc_of(row_positions, ends_ref)
            first = plan_ref[4, rb]

            @pl.loop(0, plan_ref[5, rb])
            def _(j):
                t, s = scores(block_at(keys_ref, first + j)[...], own[...])
                keep = doc_of(down((first + j) * BLOCK), ends_ref) == row_docs
                kept_t = jnp.where(keep, t, NEG_FILL)
                kept_s = jnp.where(keep, s, NEG_FILL)
                old_t = max_t[0:1]
                old_s = max_s[0:1]
                new_t = jnp.maximum(old_t, jnp.max(kept_t, axis=0, keepdims=True))
                new_s = jnp.maximum(old_s, jnp.max(kept_s, axis=0, keepdims=True))
                et = jnp.where(keep, jnp.exp2(kept_t - new_t), 0.0)
                es = jnp.where(keep, jnp.exp2(kept_s - new_s), 0.0)
                shrink_t = jnp.exp2(old_t - new_t)
                sums[0:1] = sums[0:1] * shrink_t + as_row(et)
                sums[1:2] = sums[1:2] * jnp.exp2(old_s - new_s) + as_row(es)
                sums[2:3] = sums[2:3] * shrink_t + as_row(et * (t - s))
                max_t[0:1] = new_t
                max_s[0:1] = new_s

        @pl.when(fine)
        def _():
            max_t[...] = jnp.zeros_like(max_t)
            max_s[...] = jnp.zeros_like(max_s)

        lse_t = jnp.log(sums[0:1]) + LN2 * max_t[0:1]
        lse_s = jnp.log(sums[1:2]) + LN2 * max_s[0:1]
        out_ref[rb, 0:1] = lse_t
        out_ref[rb, 1:2] = lse_s
        out_ref[rb, 2:3] = sums[2:3] * LN2 / sums[0:1] - lse_t + lse_s
        out_ref[rb, 3:4] = w_ref[rb]


def grad_kernel(rb, plan_ref, ends_ref, stats_ref, keys_ref, out_ref, row_u, acc):
    own_block = plan_ref[0, rb]
    own = block_at(keys_ref, own_block)
    top = stats_ref[0, 0:2]
    for i in range(1, 16):
        top = jnp.maximum(top, stats_ref[i, 0:2])
    calm = jnp.max(top) <= LSE_LIMIT
    acc[...] = jnp.zeros_like(acc)

    def factors(block):
        return stats_ref[block, 3:4] * jnp.exp(-stats_ref[block, 0:2])

    def tiles(first, count, keep_of):
        mine = factors(own_block)
        row_t = both_halves(as_column(mine[0:1]))
        row_s = both_halves(as_column(mine[1:2]))
        total = jnp.zeros((BLOCK, NARROW), jnp.float32)
        for j in range(count):
            key = block_at(keys_ref, first + j)
            t, s = scores(own[...], key[...])
            key_u = factors(first + j)
            symmetric = jnp.exp2(s) * (row_s + key_u[1:2]) - jnp.exp2(t) * (row_t + key_u[0:1])
            keep = keep_of(j)
            if keep is not None:
                symmetric = jnp.where(keep, symmetric, 0.0)
            total += dot(symmetric.astype(jnp.bfloat16), key[:, WIDE:], NN)
        return total

    @pl.when(jnp.logical_and(calm, plan_ref[1, rb] == 1))
    def _():
        first = plan_ref[6, 2]

        def keep_of(j):
            if 0 < j < LONG_TILES - 1:
                return None
            return within(across((first + j) * BLOCK), plan_ref)

        total = tiles(first, LONG_TILES, keep_of)
        acc[...] = jnp.where(within(down(own_block * BLOCK), plan_ref), total, 0.0)

    @pl.when(jnp.logical_and(calm, plan_ref[3, rb] > 0))
    def _():
        first = plan_ref[2, rb]
        row_docs = doc_of(down(own_block * BLOCK), ends_ref)

        def keep_of(j):
            return row_docs == doc_of(across((first + j) * BLOCK), ends_ref)

        total = tiles(first, SHORT_TILES, keep_of)
        acc[...] = jnp.where(within(down(own_block * BLOCK), plan_ref), acc[...], total)

    @pl.when(jnp.logical_not(calm))
    def _():
        for i in range(2):
            row_u[i] = as_column(stats_ref[own_block, i : i + 1] * LOG2E)
        row_u[2] = as_column(stats_ref[own_block, 3:4])
        row_docs = doc_of(down(own_block * BLOCK), ends_ref)
        first = plan_ref[4, rb]

        @pl.loop(0, plan_ref[5, rb])
        def _(j):
            key = block_at(keys_ref, first + j)
            t, s = scores(own[...], key[...])
            keep = row_docs == doc_of(across((first + j) * BLOCK), ends_ref)
            key_lse = stats_ref[first + j, 0:2] * LOG2E

            def prob(score, lse):
                return jnp.exp2(jnp.where(keep, score - lse, NEG_FILL))

            pull = both_halves(row_u[2]) * (prob(s, both_halves(row_u[1])) - prob(t, both_halves(row_u[0])))
            pull_t = stats_ref[first + j, 3:4] * (prob(s, key_lse[1:2]) - prob(t, key_lse[0:1]))
            acc[...] += dot((pull + pull_t).astype(jnp.bfloat16), key[:, WIDE:], NN)

    out_ref[...] = (acc[...] * STUDENT_SCALE).astype(out_ref.dtype)


VMEM = pl.BlockSpec(memory_space=pltpu.VMEM)
SMEM = pl.BlockSpec(memory_space=pltpu.SMEM)


def run_stats(plan, ends, w, keys):
    return pl.pallas_call(
        stats_kernel,
        out_shape=jax.ShapeDtypeStruct((4, 8, BLOCK), jnp.float32),
        in_specs=[SMEM, SMEM, VMEM, VMEM],
        out_specs=VMEM,
        scratch_shapes=[pltpu.VMEM((8, BLOCK), jnp.float32)] * 3,
        compiler_params=pltpu.CompilerParams(vmem_limit_bytes=24 * MIB),
        cost_estimate=pl.CostEstimate(flops=5 * 10**9, bytes_accessed=7 * MIB, transcendentals=0),
        name="stats",
    )(plan, ends, w, keys)


def run_grad(rb, plan, ends, stats, keys):
    return pl.pallas_call(
        functools.partial(grad_kernel, rb),
        out_shape=jax.ShapeDtypeStruct((BLOCK, NARROW), jnp.bfloat16),
        in_specs=[SMEM, SMEM, VMEM, VMEM],
        out_specs=VMEM,
        scratch_shapes=[
            pltpu.VMEM((3, BLOCK, 128), jnp.float32),
            pltpu.VMEM((BLOCK, NARROW), jnp.float32),
        ],
        compiler_params=pltpu.CompilerParams(vmem_limit_bytes=24 * MIB),
        cost_estimate=pl.CostEstimate(flops=2 * 10**9, bytes_accessed=7 * MIB, transcendentals=0),
        name="grad",
    )(plan, ends, stats, keys)


def make_plan(own_blocks, lengths, ends):
    def doc(positions):
        return jnp.sum((positions[:, None] >= ends[None, :]).astype(jnp.int32), axis=1)

    starts = ends - lengths
    longest = jnp.argmax(lengths)
    long_start, long_end = starts[longest], ends[longest]
    first_row = own_blocks * BLOCK
    last_row = first_row + (BLOCK - 1)
    lowest = starts[doc(first_row)]
    highest = ends[doc(last_row)]
    has_long = jnp.logical_and(last_row >= long_start, first_row < long_end)
    short_low = jnp.where(lowest == long_start, long_end, lowest)
    short_high = jnp.where(highest == long_end, long_start, highest)
    low_block = jnp.minimum(short_low // BLOCK, 16 - SHORT_TILES)
    short_count = jnp.where(short_high > short_low, 1, 0)
    all_low = lowest // BLOCK
    all_count = (highest + BLOCK - 1) // BLOCK - all_low
    tail = jnp.stack([long_start, long_end, jnp.minimum(long_start // BLOCK, 16 - LONG_TILES), 0])
    rows = [own_blocks, has_long, low_block, short_count, all_low, all_count, tail]
    return jnp.stack([row.astype(jnp.int32) for row in rows])


def after(value, *others):
    return lax.optimization_barrier((value,) + others)[0]


def local(teacher, student, weights, lengths):
    seq = lax.axis_index("seq")
    z, x = seq // 2, seq % 2
    c = lax.axis_index("head") % 2
    quad = z // 2

    relation = jnp.int32(0)
    for index, plane in enumerate(PLANES):
        relation = jnp.where(z == plane, index % 3, relation)
    quarters = [(k + relation) % 4 for k in range(4)]
    mine = 2 * c + x
    own_blocks = jnp.stack([q * 4 + mine for q in quarters])
    ends = jnp.cumsum(lengths)
    plan = make_plan(own_blocks, lengths, ends)

    def block(k):
        r = jnp.minimum((quad - k) % 4, 2)
        return jnp.concatenate(
            [
                lax.dynamic_index_in_dim(teacher, r, 0, False),
                lax.dynamic_index_in_dim(student, r, 0, False),
            ],
            axis=1,
        )

    def spread(pair):
        core = permute(pair, swap_pairs(0, 1))
        side = permute(pair, swap_pairs(1, 0))
        return [(0, pair), (2, core), (1, side), (3, permute(side, swap_pairs(0, 1)))]

    messages = [block(k) for k in range(4)]
    early = [permute(messages[k], out_pairs(k)) for k in range(2)]
    late = [permute(after(messages[k], *early), out_pairs(k)) for k in range(2, 4)]
    groups = [spread(jnp.concatenate(part, axis=0)) for part in (early, late)]
    w_out = after(weights.reshape(1, BLOCK), *late)
    w_rows = jnp.stack([permute(w_out, out_pairs(k)) for k in range(4)])

    keys = jnp.zeros((16 * BLOCK, WIDE + NARROW), jnp.bfloat16)
    for g, group in enumerate(groups):
        for flip, pair in group:
            for h in range(2):
                where = (quarters[2 * g + h] * 4 + (mine ^ flip)) * BLOCK
                keys = lax.dynamic_update_slice(keys, pair[h * BLOCK : (h + 1) * BLOCK], (where, 0))

    stats = run_stats(plan, ends, w_rows, keys)
    flips = ((0, stats),) + tuple(
        (2 * dc + dx, permute(stats, swap_pairs(dx, dc))) for dx, dc in ((0, 1), (1, 0), (1, 1))
    )
    all_stats = jnp.zeros((16, 8, BLOCK), jnp.float32)
    for flip, part in flips:
        for k in range(4):
            where = quarters[k] * 4 + (mine ^ flip)
            all_stats = lax.dynamic_update_slice(all_stats, part[k : k + 1], (where, 0, 0))
    grads = [run_grad(k, plan, ends, all_stats, keys) for k in range(4)]

    total = sum(permute(stats[k, 2:3], back_pairs(k)) for k in range(4))
    for flip in (1, 2, 4, 8):
        total = total + permute(
            total, [(place(z, x, g, c), place(z, x, g, c) ^ flip) for z, x, g, c in DEVICES]
        )
    row_loss = total.reshape(BLOCK)

    back = jnp.stack([permute(grads[k], back_pairs(k)) for k in range(4)])
    student_grad = jnp.stack(
        [lax.dynamic_index_in_dim(back, (quad - r) % 4, 0, False) for r in range(3)]
    ).astype(jnp.float32)
    return (row_loss, student_grad)


def solution(mesh):
    return jax.shard_map(
        local,
        mesh=mesh,
        in_specs=(P(None, "seq", "head"), P(None, "seq", "head"), P("seq"), P()),
        out_specs=(P("seq"), P(None, "seq", "head")),
        check_vma=False,
    )
```

```python
import functools
import math

import jax
import jax.numpy as jnp
from jax import lax
from jax.experimental import pallas as pl
from jax.experimental.pallas import tpu as pltpu
from jax.sharding import PartitionSpec as P

AXES = ("seq", "head")
PLANES = (0, 1, 2, 4, 5, 6)
ROUNDS = ((0, 1, 2, 3), (3, 2, 1, 0), (1, 3, 0, 2), (1, 3, 0, 2), (0, 2, 1, 3), (3, 1, 2, 0))
BLOCK = 256
WIDE = 512
NARROW = 256
LOG2E = math.log2(math.e)
LN2 = math.log(2.0)
TEACHER_SCALE = 1.0 / math.sqrt(WIDE)
STUDENT_SCALE = 1.0 / math.sqrt(NARROW)
NEG_FILL = -1e30
SUM_LIMIT = 1e30
LSE_LIMIT = 60.0
MIB = 1 << 20


def place(z, x, g, c):
    return (z * 2 + x) * 16 + g * 2 + c


DEVICES = [(z, x, g, c) for z in range(8) for x in range(2) for g in range(8) for c in range(2)]


def relation_sent(k, quarter, core):
    for r in range(3):
        if ROUNDS[core * 3 + r][k] == quarter:
            return r
    return None


def out_pairs(k):
    pairs = []
    for z, x, g, c in DEVICES:
        r = relation_sent(k, z // 2, c)
        if r is not None:
            pairs.append((place(z, x, g, c), place(PLANES[c * 3 + r], x, g, z % 2)))
    return pairs


def lookup(table, index):
    code = sum(int(value) << (2 * i) for i, value in enumerate(table))
    return lax.shift_right_logical(jnp.int32(code), (2 * index).astype(jnp.int32)) & 3


def back_pairs(k):
    return [(b, a) for a, b in out_pairs(k)]


def swap_pairs(dx, dc):
    return [(place(z, x, g, c), place(z, x ^ dx, g, c ^ dc)) for z, x, g, c in DEVICES if z in PLANES]


def permute(value, pairs):
    return lax.ppermute(value, AXES, pairs)


NT = (((1,), (1,)), ((), ()))
NN = (((1,), (0,)), ((), ()))


def dot(a, b, dims):
    return lax.dot_general(a, b, dims, preferred_element_type=jnp.float32)


def scores(rows, keys):
    t = dot(rows[:, :WIDE], keys[:, :WIDE], NT) * (TEACHER_SCALE * LOG2E)
    s = dot(rows[:, WIDE:], keys[:, WIDE:], NT) * (STUDENT_SCALE * LOG2E)
    return t, s


class Documents:
    def __init__(self, lengths_ref):
        self.starts, self.ends = [], []
        end = jnp.int32(0)
        for d in range(4):
            self.starts.append(end)
            end = end + lengths_ref[d]
            self.ends.append(end)
        self.long_start, self.long_end = self.starts[0], self.ends[0]
        for d in range(1, 4):
            longer = self.ends[d] - self.starts[d] > self.long_end - self.long_start
            self.long_start = jnp.where(longer, self.starts[d], self.long_start)
            self.long_end = jnp.where(longer, self.ends[d], self.long_end)
        self.long_block = jnp.minimum(self.long_start // BLOCK, 16 - LONG_TILES)

    def of(self, positions):
        total = jnp.zeros(positions.shape, jnp.int32)
        for end in self.ends:
            total += jnp.where(positions >= end, 1, 0)
        return total

    def in_longest(self, positions):
        return jnp.logical_and(positions >= self.long_start, positions < self.long_end)

    def of_rows(self, block):
        first = block * BLOCK
        last = first + (BLOCK - 1)
        low, high = jnp.int32(0), jnp.int32(16 * BLOCK)
        for start, end in zip(self.starts, self.ends):
            low = jnp.maximum(low, jnp.where(start <= first, start, 0))
            high = jnp.minimum(high, jnp.where(end > last, end, 16 * BLOCK))
        has_long = jnp.logical_and(last >= self.long_start, first < self.long_end)
        short_low = jnp.where(low == self.long_start, self.long_end, low)
        short_high = jnp.where(high == self.long_end, self.long_start, high)
        has_short = short_high > short_low
        short_block = jnp.minimum(short_low // BLOCK, 16 - SHORT_TILES)
        block_low = low // BLOCK
        return has_long, has_short, short_block, block_low, (high + BLOCK - 1) // BLOCK - block_low


def down(base):
    return base + lax.broadcasted_iota(jnp.int32, (BLOCK, 1), 0)


def across(base):
    return base + lax.broadcasted_iota(jnp.int32, (1, BLOCK), 1)


def fold(v):
    return jnp.sum(v.reshape(BLOCK // 8, 8, BLOCK), axis=0)


def as_row(v):
    return jnp.sum(v, axis=0, keepdims=True)


def as_column(row):
    return jnp.broadcast_to(row, (128, BLOCK)).T


def both_halves(v):
    return jnp.concatenate([v, v], axis=1)


def block_at(ref, index):
    return ref.at[pl.ds(pl.multiple_of(index * BLOCK, BLOCK), BLOCK)]


LONG_TILES = 13
SHORT_TILES = 5


def stats_kernel(lengths_ref, blocks_ref, *refs):
    own_refs, side_refs, core_ref, side_core_ref = refs[:4], refs[4:8], refs[8], refs[9]
    out_ref, keys_ref, sums, max_t, max_s = refs[10:]
    docs = Documents(lengths_ref)
    out_ref[...] = jnp.zeros_like(out_ref)
    for k in range(4):
        block = blocks_ref[k]
        part = slice(k * BLOCK, (k + 1) * BLOCK)
        quarter = block - block % 4
        place_in = block % 4
        block_at(keys_ref, block)[...] = own_refs[k][:BLOCK]
        block_at(keys_ref, quarter + (place_in ^ 1))[...] = side_refs[k][...]
        block_at(keys_ref, quarter + (place_in ^ 2))[...] = core_ref[part]
        block_at(keys_ref, quarter + (place_in ^ 3))[...] = side_core_ref[part]
        tail = own_refs[k][BLOCK:].astype(jnp.float32)
        out_ref[k, 3:4] = tail[:1, :BLOCK] + tail[:1, BLOCK : 2 * BLOCK] + tail[:1, 2 * BLOCK :]

    @pl.loop(0, 4)
    def _(rb):
        own_block = blocks_ref[rb]
        own = block_at(keys_ref, own_block)
        row_positions = across(own_block * BLOCK)
        has_long, has_short, short_block, low_block, all_blocks = docs.of_rows(own_block)
        sums[...] = jnp.zeros_like(sums)

        def gather_tiles(first, count, keep_of):
            part_t = jnp.zeros((8, BLOCK), jnp.float32)
            part_c = jnp.zeros((8, BLOCK), jnp.float32)
            part_s = jnp.zeros((8, BLOCK), jnp.float32)
            for j in range(count):
                t, s = scores(block_at(keys_ref, first + j)[...], own[...])
                et = jnp.exp2(t)
                es = jnp.exp2(s)
                keep = keep_of(j)
                if keep is not None:
                    et = jnp.where(keep, et, 0.0)
                    es = jnp.where(keep, es, 0.0)
                part_t += fold(et)
                part_s += fold(es)
                part_c += fold(et * (t - s))
            return as_row(part_t), as_row(part_s), as_row(part_c)

        @pl.when(has_long)
        def _():
            first = docs.long_block

            def keep_of(j):
                if 0 < j < LONG_TILES - 1:
                    return None
                return docs.in_longest(down((first + j) * BLOCK))

            st, ss, sc = gather_tiles(first, LONG_TILES, keep_of)
            mine = docs.in_longest(row_positions)
            sums[0:1] = jnp.where(mine, st, 0.0)
            sums[1:2] = jnp.where(mine, ss, 0.0)
            sums[2:3] = jnp.where(mine, sc, 0.0)

        @pl.when(has_short)
        def _():
            first = short_block
            row_docs = docs.of(row_positions)

            def keep_of(j):
                return docs.of(down((first + j) * BLOCK)) == row_docs

            st, ss, sc = gather_tiles(first, SHORT_TILES, keep_of)
            mine = docs.in_longest(row_positions)
            sums[0:1] = jnp.where(mine, sums[0:1], st)
            sums[1:2] = jnp.where(mine, sums[1:2], ss)
            sums[2:3] = jnp.where(mine, sums[2:3], sc)

        fine = jnp.logical_and(jnp.max(sums[0:1]) < SUM_LIMIT, jnp.max(sums[1:2]) < SUM_LIMIT)

        @pl.when(jnp.logical_not(fine))
        def _():
            sums[...] = jnp.zeros_like(sums)
            max_t[...] = jnp.full_like(max_t, NEG_FILL)
            max_s[...] = jnp.full_like(max_s, NEG_FILL)
            row_docs = docs.of(row_positions)
            first = low_block

            @pl.loop(0, all_blocks)
            def _(j):
                t, s = scores(block_at(keys_ref, first + j)[...], own[...])
                keep = docs.of(down((first + j) * BLOCK)) == row_docs
                kept_t = jnp.where(keep, t, NEG_FILL)
                kept_s = jnp.where(keep, s, NEG_FILL)
                old_t = max_t[0:1]
                old_s = max_s[0:1]
                new_t = jnp.maximum(old_t, jnp.max(kept_t, axis=0, keepdims=True))
                new_s = jnp.maximum(old_s, jnp.max(kept_s, axis=0, keepdims=True))
                et = jnp.where(keep, jnp.exp2(kept_t - new_t), 0.0)
                es = jnp.where(keep, jnp.exp2(kept_s - new_s), 0.0)
                shrink_t = jnp.exp2(old_t - new_t)
                sums[0:1] = sums[0:1] * shrink_t + as_row(et)
                sums[1:2] = sums[1:2] * jnp.exp2(old_s - new_s) + as_row(es)
                sums[2:3] = sums[2:3] * shrink_t + as_row(et * (t - s))
                max_t[0:1] = new_t
                max_s[0:1] = new_s

        @pl.when(fine)
        def _():
            max_t[...] = jnp.zeros_like(max_t)
            max_s[...] = jnp.zeros_like(max_s)

        lse_t = jnp.log(sums[0:1]) + LN2 * max_t[0:1]
        lse_s = jnp.log(sums[1:2]) + LN2 * max_s[0:1]
        out_ref[rb, 0:1] = lse_t
        out_ref[rb, 1:2] = lse_s
        out_ref[rb, 2:3] = sums[2:3] * LN2 / sums[0:1] - lse_t + lse_s


def grad_kernel(rb, lengths_ref, blocks_ref, stats_ref, keys_ref, out_ref, row_u, acc):
    docs = Documents(lengths_ref)
    own_block = blocks_ref[rb]
    has_long, has_short, short_block, low_block, all_blocks = docs.of_rows(own_block)
    own = block_at(keys_ref, own_block)
    top = stats_ref[0, 0:2]
    for i in range(1, 16):
        top = jnp.maximum(top, stats_ref[i, 0:2])
    calm = jnp.max(top) <= LSE_LIMIT
    acc[...] = jnp.zeros_like(acc)

    def factors(block):
        return stats_ref[block, 3:4] * jnp.exp(-stats_ref[block, 0:2])

    def tiles(first, count, keep_of):
        mine = factors(own_block)
        row_t = both_halves(as_column(mine[0:1]))
        row_s = both_halves(as_column(mine[1:2]))
        total = jnp.zeros((BLOCK, NARROW), jnp.float32)
        for j in range(count):
            key = block_at(keys_ref, first + j)
            t, s = scores(own[...], key[...])
            key_u = factors(first + j)
            symmetric = jnp.exp2(s) * (row_s + key_u[1:2]) - jnp.exp2(t) * (row_t + key_u[0:1])
            keep = keep_of(j)
            if keep is not None:
                symmetric = jnp.where(keep, symmetric, 0.0)
            total += dot(symmetric.astype(jnp.bfloat16), key[:, WIDE:], NN)
        return total

    @pl.when(jnp.logical_and(calm, has_long))
    def _():
        first = docs.long_block

        def keep_of(j):
            if 0 < j < LONG_TILES - 1:
                return None
            return docs.in_longest(across((first + j) * BLOCK))

        total = tiles(first, LONG_TILES, keep_of)
        acc[...] = jnp.where(docs.in_longest(down(own_block * BLOCK)), total, 0.0)

    @pl.when(jnp.logical_and(calm, has_short))
    def _():
        first = short_block
        row_docs = docs.of(down(own_block * BLOCK))

        def keep_of(j):
            return row_docs == docs.of(across((first + j) * BLOCK))

        total = tiles(first, SHORT_TILES, keep_of)
        acc[...] = jnp.where(docs.in_longest(down(own_block * BLOCK)), acc[...], total)

    @pl.when(jnp.logical_not(calm))
    def _():
        for i in range(2):
            row_u[i] = as_column(stats_ref[own_block, i : i + 1] * LOG2E)
        row_u[2] = as_column(stats_ref[own_block, 3:4])
        row_docs = docs.of(down(own_block * BLOCK))
        first = low_block

        @pl.loop(0, all_blocks)
        def _(j):
            key = block_at(keys_ref, first + j)
            t, s = scores(own[...], key[...])
            keep = row_docs == docs.of(across((first + j) * BLOCK))
            key_lse = stats_ref[first + j, 0:2] * LOG2E

            def prob(score, lse):
                return jnp.exp2(jnp.where(keep, score - lse, NEG_FILL))

            pull = both_halves(row_u[2]) * (prob(s, both_halves(row_u[1])) - prob(t, both_halves(row_u[0])))
            pull_t = stats_ref[first + j, 3:4] * (prob(s, key_lse[1:2]) - prob(t, key_lse[0:1]))
            acc[...] += dot((pull + pull_t).astype(jnp.bfloat16), key[:, WIDE:], NN)

    out_ref[...] = (acc[...] * STUDENT_SCALE).astype(out_ref.dtype)


VMEM = pl.BlockSpec(memory_space=pltpu.VMEM)
SMEM = pl.BlockSpec(memory_space=pltpu.SMEM)


def run_stats(lengths, blocks, pieces):
    return pl.pallas_call(
        stats_kernel,
        out_shape=(
            jax.ShapeDtypeStruct((4, 8, BLOCK), jnp.float32),
            jax.ShapeDtypeStruct((16 * BLOCK, WIDE + NARROW), jnp.bfloat16),
        ),
        in_specs=[SMEM, SMEM] + [VMEM] * 10,
        out_specs=(VMEM, VMEM),
        scratch_shapes=[pltpu.VMEM((8, BLOCK), jnp.float32)] * 3,
        compiler_params=pltpu.CompilerParams(vmem_limit_bytes=24 * MIB),
        cost_estimate=pl.CostEstimate(flops=5 * 10**9, bytes_accessed=7 * MIB, transcendentals=0),
        name="stats",
    )(lengths, blocks, *pieces)


def run_grad(rb, lengths, blocks, stats, keys):
    return pl.pallas_call(
        functools.partial(grad_kernel, rb),
        out_shape=jax.ShapeDtypeStruct((BLOCK, NARROW), jnp.bfloat16),
        in_specs=[SMEM, SMEM, VMEM, VMEM],
        out_specs=VMEM,
        scratch_shapes=[
            pltpu.VMEM((3, BLOCK, 128), jnp.float32),
            pltpu.VMEM((BLOCK, NARROW), jnp.float32),
        ],
        compiler_params=pltpu.CompilerParams(vmem_limit_bytes=16 * MIB),
        cost_estimate=pl.CostEstimate(flops=2 * 10**9, bytes_accessed=7 * MIB, transcendentals=0),
        name="grad",
    )(lengths, blocks, stats, keys)


def after(value, *others):
    return lax.optimization_barrier((value,) + others)[0]


def in_thirds(row):
    high = lax.reduce_precision(row, 8, 7)
    middle = lax.reduce_precision(row - high, 8, 7)
    return [part.astype(jnp.bfloat16) for part in (high, middle, row - high - middle)]


def local(teacher, student, weights, lengths):
    seq = lax.axis_index("seq")
    z, x = seq // 2, seq % 2
    head = lax.axis_index("head")
    c = head % 2
    source = (z // 2) * 2 + c

    items = [ROUNDS[PLANES.index(p)] if p in PLANES else (0, 1, 2, 3) for p in range(8)]
    quarters = [lookup([items[p][k] for p in range(8)], z) for k in range(4)]
    mine = 2 * c + x
    blocks = jnp.stack([q * 4 + mine for q in quarters])

    w_tail = jnp.concatenate(in_thirds(weights.reshape(1, BLOCK)), axis=1)
    w_tail = jnp.pad(w_tail, ((0, 15), (0, 0)))

    def message(k):
        sent = [relation_sent(k, q, core) or 0 for q in range(4) for core in range(2)]
        r = lookup(sent, source)
        vectors = [lax.dynamic_index_in_dim(v, r, 0, False) for v in (teacher, student)]
        return jnp.concatenate([jnp.concatenate(vectors, axis=1), w_tail], axis=0)

    own = [permute(message(k), out_pairs(k)) for k in range(4)]
    mine_only = [v[:BLOCK] for v in own]
    side = [permute(v, swap_pairs(1, 0)) for v in mine_only]
    core = permute(after(jnp.concatenate(mine_only, axis=0), side[1]), swap_pairs(0, 1))
    side_core = permute(jnp.concatenate(side, axis=0), swap_pairs(0, 1))

    stats, keys = run_stats(lengths, blocks, own + side + [core, side_core])

    flips = ((0, stats),) + tuple(
        (2 * dc + dx, permute(stats, swap_pairs(dx, dc))) for dx, dc in ((0, 1), (1, 0), (1, 1))
    )
    all_stats = jnp.zeros((16, 8, BLOCK), jnp.float32)
    for flip, part in flips:
        for k in range(4):
            where = quarters[k] * 4 + (mine ^ flip)
            all_stats = lax.dynamic_update_slice(all_stats, part[k : k + 1], (where, 0, 0))
    grads = [run_grad(k, lengths, blocks, all_stats, keys) for k in range(4)]

    loss = after(stats[:, 2], all_stats)
    for flip in (2, 4, 8):
        loss = loss + permute(
            loss, [(place(z, x, g, c), place(z, x, g, c) ^ flip) for z, x, g, c in DEVICES]
        )

    back = []
    for k in range(4):
        tail = jnp.concatenate(in_thirds(loss[k : k + 1]), axis=0)
        tail = jnp.pad(tail, ((0, 13), (0, 0)))
        back.append(permute(jnp.concatenate([grads[k], tail], axis=0), back_pairs(k)))
    total = sum(v[BLOCK : BLOCK + 3].astype(jnp.float32) for v in back)
    total = jnp.sum(total, axis=0, keepdims=True)
    total = total + permute(
        total, [(place(z, x, g, c), place(z, x, g, c) ^ 1) for z, x, g, c in DEVICES]
    )
    row_loss = total.reshape(BLOCK)

    back = jnp.stack([v[:BLOCK] for v in back])
    came = []
    for r in range(3):
        table = [ROUNDS[core * 3 + r].index(q) for q in range(4) for core in range(2)]
        came.append(lax.dynamic_index_in_dim(back, lookup(table, source), 0, False))
    return (row_loss, jnp.stack(came).astype(jnp.float32))


def solution(mesh):
    return jax.shard_map(
        local,
        mesh=mesh,
        in_specs=(P(None, "seq", "head"), P(None, "seq", "head"), P("seq"), P()),
        out_specs=(P("seq"), P(None, "seq", "head")),
        check_vma=False,
    )
```

```python
import functools
import math

import jax
import jax.numpy as jnp
from jax import lax
from jax.experimental import pallas as pl
from jax.experimental.pallas import tpu as pltpu
from jax.sharding import PartitionSpec as P

AXES = ("seq", "head")
PLANES = (0, 1, 2, 4, 5, 6)
ROUNDS = ((0, 1, 2, 3), (3, 2, 1, 0), (1, 3, 0, 2), (1, 3, 0, 2), (0, 2, 1, 3), (3, 1, 2, 0))
BLOCK = 256
WIDE = 512
NARROW = 256
LOG2E = math.log2(math.e)
LN2 = math.log(2.0)
TEACHER_SCALE = 1.0 / math.sqrt(WIDE)
STUDENT_SCALE = 1.0 / math.sqrt(NARROW)
NEG_FILL = -1e30
SUM_LIMIT = 1e30
LSE_LIMIT = 60.0
MIB = 1 << 20


def place(z, x, g, c):
    return (z * 2 + x) * 16 + g * 2 + c


DEVICES = [(z, x, g, c) for z in range(8) for x in range(2) for g in range(8) for c in range(2)]


def relation_sent(k, quarter, core):
    for r in range(3):
        if ROUNDS[core * 3 + r][k] == quarter:
            return r
    return None


def out_pairs(k):
    pairs = []
    for z, x, g, c in DEVICES:
        r = relation_sent(k, z // 2, c)
        if r is not None:
            pairs.append((place(z, x, g, c), place(PLANES[c * 3 + r], x, g, z % 2)))
    return pairs


def lookup(table, index):
    code = sum(int(value) << (2 * i) for i, value in enumerate(table))
    return lax.shift_right_logical(jnp.int32(code), (2 * index).astype(jnp.int32)) & 3


def back_pairs(k):
    return [(b, a) for a, b in out_pairs(k)]


def swap_pairs(dx, dc):
    return [(place(z, x, g, c), place(z, x ^ dx, g, c ^ dc)) for z, x, g, c in DEVICES if z in PLANES]


def permute(value, pairs):
    return lax.ppermute(value, AXES, pairs)


NT = (((1,), (1,)), ((), ()))
NN = (((1,), (0,)), ((), ()))


def dot(a, b, dims):
    return lax.dot_general(a, b, dims, preferred_element_type=jnp.float32)


def scores(rows, keys):
    t = dot(rows[:, :WIDE], keys[:, :WIDE], NT) * (TEACHER_SCALE * LOG2E)
    s = dot(rows[:, WIDE:], keys[:, WIDE:], NT) * (STUDENT_SCALE * LOG2E)
    return t, s


class Documents:
    def __init__(self, lengths_ref):
        self.starts, self.ends = [], []
        end = jnp.int32(0)
        for d in range(4):
            self.starts.append(end)
            end = end + lengths_ref[d]
            self.ends.append(end)
        self.long_start, self.long_end = self.starts[0], self.ends[0]
        for d in range(1, 4):
            longer = self.ends[d] - self.starts[d] > self.long_end - self.long_start
            self.long_start = jnp.where(longer, self.starts[d], self.long_start)
            self.long_end = jnp.where(longer, self.ends[d], self.long_end)
        self.long_block = jnp.minimum(self.long_start // BLOCK, 16 - LONG_TILES)

    def of(self, positions):
        total = jnp.zeros(positions.shape, jnp.int32)
        for end in self.ends:
            total += jnp.where(positions >= end, 1, 0)
        return total

    def in_longest(self, positions):
        return jnp.logical_and(positions >= self.long_start, positions < self.long_end)

    def of_rows(self, block):
        first = block * BLOCK
        last = first + (BLOCK - 1)
        low, high = jnp.int32(0), jnp.int32(16 * BLOCK)
        for start, end in zip(self.starts, self.ends):
            low = jnp.maximum(low, jnp.where(start <= first, start, 0))
            high = jnp.minimum(high, jnp.where(end > last, end, 16 * BLOCK))
        has_long = jnp.logical_and(last >= self.long_start, first < self.long_end)
        short_low = jnp.where(low == self.long_start, self.long_end, low)
        short_high = jnp.where(high == self.long_end, self.long_start, high)
        has_short = short_high > short_low
        short_block = jnp.minimum(short_low // BLOCK, 16 - SHORT_TILES)
        block_low = low // BLOCK
        return has_long, has_short, short_block, block_low, (high + BLOCK - 1) // BLOCK - block_low


def down(base):
    return base + lax.broadcasted_iota(jnp.int32, (BLOCK, 1), 0)


def across(base):
    return base + lax.broadcasted_iota(jnp.int32, (1, BLOCK), 1)


def fold(v):
    return jnp.sum(v.reshape(BLOCK // 8, 8, BLOCK), axis=0)


def as_row(v):
    return jnp.sum(v, axis=0, keepdims=True)


def as_column(row):
    return jnp.broadcast_to(row, (128, BLOCK)).T


def both_halves(v):
    return jnp.concatenate([v, v], axis=1)


def block_at(ref, index):
    return ref.at[pl.ds(pl.multiple_of(index * BLOCK, BLOCK), BLOCK)]


LONG_TILES = 13
SHORT_TILES = 5


def stats_kernel(lengths_ref, blocks_ref, *refs):
    own_refs, side_refs, core_ref, side_core_refs = refs[:4], refs[4:8], refs[8], refs[9:11]
    out_ref, loss_ref, keys_ref, sums, max_t, max_s = refs[11:]
    docs = Documents(lengths_ref)
    out_ref[...] = jnp.zeros_like(out_ref)
    for k in range(4):
        block = blocks_ref[k]
        part = slice(k * BLOCK, (k + 1) * BLOCK)
        quarter = block - block % 4
        place_in = block % 4
        block_at(keys_ref, block)[...] = own_refs[k][:BLOCK]
        block_at(keys_ref, quarter + (place_in ^ 1))[...] = side_refs[k][...]
        block_at(keys_ref, quarter + (place_in ^ 2))[...] = core_ref[part]
        far = side_core_refs[0][part] if k < 3 else side_core_refs[1][...]
        block_at(keys_ref, quarter + (place_in ^ 3))[...] = far
        tail = own_refs[k][BLOCK:].astype(jnp.float32)
        out_ref[k, 3:4] = tail[:1, :BLOCK] + tail[:1, BLOCK : 2 * BLOCK] + tail[:1, 2 * BLOCK :]

    @pl.loop(0, 4)
    def _(rb):
        own_block = blocks_ref[rb]
        own = block_at(keys_ref, own_block)
        row_positions = across(own_block * BLOCK)
        has_long, has_short, short_block, low_block, all_blocks = docs.of_rows(own_block)
        sums[...] = jnp.zeros_like(sums)

        def gather_tiles(first, count, keep_of):
            part_t = jnp.zeros((8, BLOCK), jnp.float32)
            part_c = jnp.zeros((8, BLOCK), jnp.float32)
            part_s = jnp.zeros((8, BLOCK), jnp.float32)
            for j in range(count):
                t, s = scores(block_at(keys_ref, first + j)[...], own[...])
                et = jnp.exp2(t)
                es = jnp.exp2(s)
                keep = keep_of(j)
                if keep is not None:
                    et = jnp.where(keep, et, 0.0)
                    es = jnp.where(keep, es, 0.0)
                part_t += fold(et)
                part_s += fold(es)
                part_c += fold(et * (t - s))
            return as_row(part_t), as_row(part_s), as_row(part_c)

        @pl.when(has_long)
        def _():
            first = docs.long_block

            def keep_of(j):
                if 0 < j < LONG_TILES - 1:
                    return None
                return docs.in_longest(down((first + j) * BLOCK))

            st, ss, sc = gather_tiles(first, LONG_TILES, keep_of)
            mine = docs.in_longest(row_positions)
            sums[0:1] = jnp.where(mine, st, 0.0)
            sums[1:2] = jnp.where(mine, ss, 0.0)
            sums[2:3] = jnp.where(mine, sc, 0.0)

        @pl.when(has_short)
        def _():
            first = short_block
            row_docs = docs.of(row_positions)

            def keep_of(j):
                return docs.of(down((first + j) * BLOCK)) == row_docs

            st, ss, sc = gather_tiles(first, SHORT_TILES, keep_of)
            mine = docs.in_longest(row_positions)
            sums[0:1] = jnp.where(mine, sums[0:1], st)
            sums[1:2] = jnp.where(mine, sums[1:2], ss)
            sums[2:3] = jnp.where(mine, sums[2:3], sc)

        fine = jnp.logical_and(jnp.max(sums[0:1]) < SUM_LIMIT, jnp.max(sums[1:2]) < SUM_LIMIT)

        @pl.when(jnp.logical_not(fine))
        def _():
            sums[...] = jnp.zeros_like(sums)
            max_t[...] = jnp.full_like(max_t, NEG_FILL)
            max_s[...] = jnp.full_like(max_s, NEG_FILL)
            row_docs = docs.of(row_positions)
            first = low_block

            @pl.loop(0, all_blocks)
            def _(j):
                t, s = scores(block_at(keys_ref, first + j)[...], own[...])
                keep = docs.of(down((first + j) * BLOCK)) == row_docs
                kept_t = jnp.where(keep, t, NEG_FILL)
                kept_s = jnp.where(keep, s, NEG_FILL)
                old_t = max_t[0:1]
                old_s = max_s[0:1]
                new_t = jnp.maximum(old_t, jnp.max(kept_t, axis=0, keepdims=True))
                new_s = jnp.maximum(old_s, jnp.max(kept_s, axis=0, keepdims=True))
                et = jnp.where(keep, jnp.exp2(kept_t - new_t), 0.0)
                es = jnp.where(keep, jnp.exp2(kept_s - new_s), 0.0)
                shrink_t = jnp.exp2(old_t - new_t)
                sums[0:1] = sums[0:1] * shrink_t + as_row(et)
                sums[1:2] = sums[1:2] * jnp.exp2(old_s - new_s) + as_row(es)
                sums[2:3] = sums[2:3] * shrink_t + as_row(et * (t - s))
                max_t[0:1] = new_t
                max_s[0:1] = new_s

        @pl.when(fine)
        def _():
            max_t[...] = jnp.zeros_like(max_t)
            max_s[...] = jnp.zeros_like(max_s)

        lse_t = jnp.log(sums[0:1]) + LN2 * max_t[0:1]
        lse_s = jnp.log(sums[1:2]) + LN2 * max_s[0:1]
        out_ref[rb, 0:1] = lse_t
        out_ref[rb, 1:2] = lse_s
        loss_ref[pl.ds(own_block // 4, 1)] = sums[2:3] * LN2 / sums[0:1] - lse_t + lse_s


def grad_kernel(rb, lengths_ref, blocks_ref, stats_ref, keys_ref, out_ref, row_u, acc):
    docs = Documents(lengths_ref)
    own_block = blocks_ref[rb]
    has_long, has_short, short_block, low_block, all_blocks = docs.of_rows(own_block)
    own = block_at(keys_ref, own_block)
    top = stats_ref[0, 0:2]
    for i in range(1, 16):
        top = jnp.maximum(top, stats_ref[i, 0:2])
    calm = jnp.max(top) <= LSE_LIMIT
    acc[...] = jnp.zeros_like(acc)

    def factors(block):
        return stats_ref[block, 3:4] * jnp.exp(-stats_ref[block, 0:2])

    def tiles(first, count, keep_of):
        mine = factors(own_block)
        row_t = both_halves(as_column(mine[0:1]))
        row_s = both_halves(as_column(mine[1:2]))
        total = jnp.zeros((BLOCK, NARROW), jnp.float32)
        for j in range(count):
            key = block_at(keys_ref, first + j)
            t, s = scores(own[...], key[...])
            key_u = factors(first + j)
            symmetric = jnp.exp2(s) * (row_s + key_u[1:2]) - jnp.exp2(t) * (row_t + key_u[0:1])
            keep = keep_of(j)
            if keep is not None:
                symmetric = jnp.where(keep, symmetric, 0.0)
            total += dot(symmetric.astype(jnp.bfloat16), key[:, WIDE:], NN)
        return total

    @pl.when(jnp.logical_and(calm, has_long))
    def _():
        first = docs.long_block

        def keep_of(j):
            if 0 < j < LONG_TILES - 1:
                return None
            return docs.in_longest(across((first + j) * BLOCK))

        total = tiles(first, LONG_TILES, keep_of)
        acc[...] = jnp.where(docs.in_longest(down(own_block * BLOCK)), total, 0.0)

    @pl.when(jnp.logical_and(calm, has_short))
    def _():
        first = short_block
        row_docs = docs.of(down(own_block * BLOCK))

        def keep_of(j):
            return row_docs == docs.of(across((first + j) * BLOCK))

        total = tiles(first, SHORT_TILES, keep_of)
        acc[...] = jnp.where(docs.in_longest(down(own_block * BLOCK)), acc[...], total)

    @pl.when(jnp.logical_not(calm))
    def _():
        for i in range(2):
            row_u[i] = as_column(stats_ref[own_block, i : i + 1] * LOG2E)
        row_u[2] = as_column(stats_ref[own_block, 3:4])
        row_docs = docs.of(down(own_block * BLOCK))
        first = low_block

        @pl.loop(0, all_blocks)
        def _(j):
            key = block_at(keys_ref, first + j)
            t, s = scores(own[...], key[...])
            keep = row_docs == docs.of(across((first + j) * BLOCK))
            key_lse = stats_ref[first + j, 0:2] * LOG2E

            def prob(score, lse):
                return jnp.exp2(jnp.where(keep, score - lse, NEG_FILL))

            pull = both_halves(row_u[2]) * (prob(s, both_halves(row_u[1])) - prob(t, both_halves(row_u[0])))
            pull_t = stats_ref[first + j, 3:4] * (prob(s, key_lse[1:2]) - prob(t, key_lse[0:1]))
            acc[...] += dot((pull + pull_t).astype(jnp.bfloat16), key[:, WIDE:], NN)

    out_ref[...] = (acc[...] * STUDENT_SCALE).astype(out_ref.dtype)


VMEM = pl.BlockSpec(memory_space=pltpu.VMEM)
SMEM = pl.BlockSpec(memory_space=pltpu.SMEM)


def run_stats(lengths, blocks, pieces):
    return pl.pallas_call(
        stats_kernel,
        out_shape=(
            jax.ShapeDtypeStruct((4, 8, BLOCK), jnp.float32),
            jax.ShapeDtypeStruct((4, BLOCK), jnp.float32),
            jax.ShapeDtypeStruct((16 * BLOCK, WIDE + NARROW), jnp.bfloat16),
        ),
        in_specs=[SMEM, SMEM] + [VMEM] * 11,
        out_specs=(VMEM, VMEM, VMEM),
        scratch_shapes=[pltpu.VMEM((8, BLOCK), jnp.float32)] * 3,
        compiler_params=pltpu.CompilerParams(vmem_limit_bytes=24 * MIB),
        cost_estimate=pl.CostEstimate(flops=5 * 10**9, bytes_accessed=7 * MIB, transcendentals=0),
        name="stats",
    )(lengths, blocks, *pieces)


def run_grad(rb, lengths, blocks, stats, keys):
    return pl.pallas_call(
        functools.partial(grad_kernel, rb),
        out_shape=jax.ShapeDtypeStruct((BLOCK, NARROW), jnp.bfloat16),
        in_specs=[SMEM, SMEM, VMEM, VMEM],
        out_specs=VMEM,
        scratch_shapes=[
            pltpu.VMEM((3, BLOCK, 128), jnp.float32),
            pltpu.VMEM((BLOCK, NARROW), jnp.float32),
        ],
        compiler_params=pltpu.CompilerParams(vmem_limit_bytes=16 * MIB),
        cost_estimate=pl.CostEstimate(flops=2 * 10**9, bytes_accessed=7 * MIB, transcendentals=0),
        name="grad",
    )(lengths, blocks, stats, keys)


def after(value, *others):
    return lax.optimization_barrier((value,) + others)[0]


def in_thirds(row):
    high = lax.reduce_precision(row, 8, 7)
    middle = lax.reduce_precision(row - high, 8, 7)
    return [part.astype(jnp.bfloat16) for part in (high, middle, row - high - middle)]


def local(teacher, student, weights, lengths):
    seq = lax.axis_index("seq")
    z, x = seq // 2, seq % 2
    head = lax.axis_index("head")
    c = head % 2
    source = (z // 2) * 2 + c

    items = [ROUNDS[PLANES.index(p)] if p in PLANES else (0, 1, 2, 3) for p in range(8)]
    quarters = [lookup([items[p][k] for p in range(8)], z) for k in range(4)]
    mine = 2 * c + x
    blocks = jnp.stack([q * 4 + mine for q in quarters])

    w_tail = jnp.concatenate(in_thirds(weights.reshape(1, BLOCK)), axis=1)
    w_tail = jnp.pad(w_tail, ((0, 15), (0, 0)))

    def message(k):
        sent = [relation_sent(k, q, core) or 0 for q in range(4) for core in range(2)]
        r = lookup(sent, source)
        vectors = [lax.dynamic_index_in_dim(v, r, 0, False) for v in (teacher, student)]
        return jnp.concatenate([jnp.concatenate(vectors, axis=1), w_tail], axis=0)

    own = [permute(message(k), out_pairs(k)) for k in range(4)]
    mine_only = [v[:BLOCK] for v in own]
    core = permute(jnp.concatenate(mine_only, axis=0), swap_pairs(0, 1))
    side = [permute(v, swap_pairs(1, 0)) for v in mine_only[:3]]
    side.append(permute(after(mine_only[3], core), swap_pairs(1, 0)))
    side_core = [
        permute(v, swap_pairs(0, 1)) for v in (jnp.concatenate(side[:3], axis=0), side[3])
    ]

    stats, loss, keys = run_stats(lengths, blocks, own + side + [core] + side_core)

    both = jnp.stack([stats, permute(stats, swap_pairs(1, 0))])
    four = [both, permute(both, swap_pairs(0, 1))]
    all_stats = jnp.zeros((16, 8, BLOCK), jnp.float32)
    for flip in range(4):
        for k in range(4):
            where = quarters[k] * 4 + (mine ^ flip)
            all_stats = lax.dynamic_update_slice(
                all_stats, four[flip // 2][flip % 2, k : k + 1], (where, 0, 0)
            )
    grads = []
    for step, (dz, dh) in enumerate(((4, 0), (0, 2), (0, 4), (0, 8))):
        pairs = [(place(z, x, g, c), place(z ^ dz, x, g, c) ^ dh) for z, x, g, c in DEVICES]
        if step == 1:
            loss = after(loss, all_stats)
        elif step > 1:
            loss = after(loss, grads[step - 2])
        came = permute(loss, pairs)
        if step > 0:
            grads.append(run_grad(step - 1, lengths, blocks, all_stats, keys))
        loss = loss + came
        blocks = after(blocks, loss)
    grads.append(run_grad(3, lengths, blocks, all_stats, keys))

    back = []
    for k in range(4):
        tail = jnp.concatenate(in_thirds(lax.dynamic_slice_in_dim(loss, quarters[k], 1, 0)), axis=0)
        tail = jnp.pad(tail, ((0, 13), (0, 0)))
        back.append(permute(jnp.concatenate([grads[k], tail], axis=0), back_pairs(k)))
    total = sum(v[BLOCK : BLOCK + 3].astype(jnp.float32) for v in back)
    row_loss = jnp.sum(total, axis=0)

    back = jnp.stack([v[:BLOCK] for v in back])
    came = []
    for r in range(3):
        table = [ROUNDS[core * 3 + r].index(q) for q in range(4) for core in range(2)]
        came.append(lax.dynamic_index_in_dim(back, lookup(table, source), 0, False))
    return (row_loss, jnp.stack(came).astype(jnp.float32))


def solution(mesh):
    return jax.shard_map(
        local,
        mesh=mesh,
        in_specs=(P(None, "seq", "head"), P(None, "seq", "head"), P("seq"), P()),
        out_specs=(P("seq"), P(None, "seq", "head")),
        check_vma=False,
    )
```

```python
import functools
import math

import jax
import jax.numpy as jnp
from jax import lax
from jax.experimental import pallas as pl
from jax.experimental.pallas import tpu as pltpu
from jax.sharding import PartitionSpec as P

AXES = ("seq", "head")
PLANES = (0, 1, 2, 4, 5, 6)
ROUNDS = ((0, 1, 2, 3), (3, 2, 1, 0), (1, 3, 0, 2), (1, 3, 0, 2), (0, 2, 1, 3), (3, 1, 2, 0))
BLOCK = 256
WIDE = 512
NARROW = 256
LOG2E = math.log2(math.e)
LN2 = math.log(2.0)
TEACHER_SCALE = 1.0 / math.sqrt(WIDE)
STUDENT_SCALE = 1.0 / math.sqrt(NARROW)
NEG_FILL = -1e30
SUM_LIMIT = 1e30
LSE_LIMIT = 60.0
MIB = 1 << 20


def place(z, x, g, c):
    return (z * 2 + x) * 16 + g * 2 + c


DEVICES = [(z, x, g, c) for z in range(8) for x in range(2) for g in range(8) for c in range(2)]


def relation_sent(k, quarter, core):
    for r in range(3):
        if ROUNDS[core * 3 + r][k] == quarter:
            return r
    return None


def out_pairs(k):
    pairs = []
    for z, x, g, c in DEVICES:
        r = relation_sent(k, z // 2, c)
        if r is not None:
            pairs.append((place(z, x, g, c), place(PLANES[c * 3 + r], x, g, z % 2)))
    return pairs


def lookup(table, index):
    code = sum(int(value) << (2 * i) for i, value in enumerate(table))
    return lax.shift_right_logical(jnp.int32(code), (2 * index).astype(jnp.int32)) & 3


def back_pairs(k):
    return [(b, a) for a, b in out_pairs(k)]


def swap_pairs(dx, dc):
    return [(place(z, x, g, c), place(z, x ^ dx, g, c ^ dc)) for z, x, g, c in DEVICES if z in PLANES]


def permute(value, pairs):
    return lax.ppermute(value, AXES, pairs)


NT = (((1,), (1,)), ((), ()))
NN = (((1,), (0,)), ((), ()))


def dot(a, b, dims):
    return lax.dot_general(a, b, dims, preferred_element_type=jnp.float32)


def scores(rows, keys):
    t = dot(rows[:, :WIDE], keys[:, :WIDE], NT) * (TEACHER_SCALE * LOG2E)
    s = dot(rows[:, WIDE:], keys[:, WIDE:], NT) * (STUDENT_SCALE * LOG2E)
    return t, s


class Documents:
    def __init__(self, lengths_ref):
        self.starts, self.ends = [], []
        end = jnp.int32(0)
        for d in range(4):
            self.starts.append(end)
            end = end + lengths_ref[d]
            self.ends.append(end)
        self.long_start, self.long_end = self.starts[0], self.ends[0]
        for d in range(1, 4):
            longer = self.ends[d] - self.starts[d] > self.long_end - self.long_start
            self.long_start = jnp.where(longer, self.starts[d], self.long_start)
            self.long_end = jnp.where(longer, self.ends[d], self.long_end)
        self.long_block = jnp.minimum(self.long_start // BLOCK, 16 - LONG_TILES)

    def of(self, positions):
        total = jnp.zeros(positions.shape, jnp.int32)
        for end in self.ends:
            total += jnp.where(positions >= end, 1, 0)
        return total

    def in_longest(self, positions):
        return jnp.logical_and(positions >= self.long_start, positions < self.long_end)

    def of_rows(self, block):
        first = block * BLOCK
        last = first + (BLOCK - 1)
        low, high = jnp.int32(0), jnp.int32(16 * BLOCK)
        for start, end in zip(self.starts, self.ends):
            low = jnp.maximum(low, jnp.where(start <= first, start, 0))
            high = jnp.minimum(high, jnp.where(end > last, end, 16 * BLOCK))
        has_long = jnp.logical_and(last >= self.long_start, first < self.long_end)
        short_low = jnp.where(low == self.long_start, self.long_end, low)
        short_high = jnp.where(high == self.long_end, self.long_start, high)
        has_short = short_high > short_low
        short_block = jnp.minimum(short_low // BLOCK, 16 - SHORT_TILES)
        block_low = low // BLOCK
        return has_long, has_short, short_block, block_low, (high + BLOCK - 1) // BLOCK - block_low


def down(base):
    return base + lax.broadcasted_iota(jnp.int32, (BLOCK, 1), 0)


def across(base):
    return base + lax.broadcasted_iota(jnp.int32, (1, BLOCK), 1)


def fold(v):
    return jnp.sum(v.reshape(BLOCK // 8, 8, BLOCK), axis=0)


def as_row(v):
    return jnp.sum(v, axis=0, keepdims=True)


def as_column(row):
    return jnp.broadcast_to(row, (128, BLOCK)).T


def both_halves(v):
    return jnp.concatenate([v, v], axis=1)


def block_at(ref, index):
    return ref.at[pl.ds(pl.multiple_of(index * BLOCK, BLOCK), BLOCK)]


LONG_TILES = 13
SHORT_TILES = 5
LONG_HALF = 7
SHORT_HALF = 3


def half_block(index, half):
    return (index // 2) * 4 + 2 * half + index % 2


def half_window(first, half, count):
    inside = jnp.bitwise_and(first // 2, 1) == half
    low = jnp.where(inside, first % 2, jnp.where(half == 1, 0, 2))
    return jnp.minimum((first // 4) * 2 + low, 8 - count)


def add_half(docs, own_block, half, own, key_at, sums):
    row_positions = across(own_block * BLOCK)
    has_long, has_short, short_block, _, _ = docs.of_rows(own_block)

    def tiles(first, count, keep_of):
        part_t = jnp.zeros((8, BLOCK), jnp.float32)
        part_c = jnp.zeros((8, BLOCK), jnp.float32)
        part_s = jnp.zeros((8, BLOCK), jnp.float32)
        for j in range(count):
            t, s = scores(key_at(first + j)[...], own[...])
            et = jnp.exp2(t)
            es = jnp.exp2(s)
            keep = keep_of(j, down(half_block(first + j, half) * BLOCK))
            if keep is not None:
                et = jnp.where(keep, et, 0.0)
                es = jnp.where(keep, es, 0.0)
            part_t += fold(et)
            part_s += fold(es)
            part_c += fold(et * (t - s))
        return as_row(part_t), as_row(part_s), as_row(part_c)

    def add(parts, rows):
        for i, part in enumerate(parts):
            sums[i : i + 1] += jnp.where(rows, part, 0.0)

    @pl.when(has_long)
    def _():
        first = half_window(docs.long_start // BLOCK, half, LONG_HALF)

        def keep_of(j, positions):
            return None if 0 < j < LONG_HALF - 1 else docs.in_longest(positions)

        add(tiles(first, LONG_HALF, keep_of), docs.in_longest(row_positions))

    @pl.when(has_short)
    def _():
        first = half_window(short_block, half, SHORT_HALF)
        row_docs = docs.of(row_positions)

        def keep_of(j, positions):
            return docs.of(positions) == row_docs

        add(tiles(first, SHORT_HALF, keep_of), jnp.logical_not(docs.in_longest(row_positions)))


def early_kernel(lengths_ref, blocks_ref, *refs):
    own_refs, side_refs, out_ref, half_ref, sums = refs[:4], refs[4:8], refs[8], refs[9], refs[10]
    docs = Documents(lengths_ref)
    half = jnp.bitwise_and(blocks_ref[0] // 2, 1)
    out_ref[...] = jnp.zeros_like(out_ref)
    for k in range(4):
        index = (blocks_ref[k] // 4) * 2 + blocks_ref[k] % 2
        block_at(half_ref, index)[...] = own_refs[k][:BLOCK]
        block_at(half_ref, jnp.bitwise_xor(index, 1))[...] = side_refs[k][...]
        tail = own_refs[k][BLOCK:].astype(jnp.float32)
        out_ref[k, 3:4] = tail[:1, :BLOCK] + tail[:1, BLOCK : 2 * BLOCK] + tail[:1, 2 * BLOCK :]

    @pl.loop(0, 4)
    def _(rb):
        own_block = blocks_ref[rb]
        sums[...] = jnp.zeros_like(sums)
        own = block_at(half_ref, (own_block // 4) * 2 + own_block % 2)
        add_half(docs, own_block, half, own, functools.partial(block_at, half_ref), sums)
        out_ref[rb, 0:3] = sums[0:3]


def stats_kernel(lengths_ref, blocks_ref, part_ref, half_ref, core_ref, far_ref, *refs):
    out_ref, loss_ref, keys_ref, sums, max_t, max_s = refs
    docs = Documents(lengths_ref)
    half = jnp.bitwise_and(blocks_ref[0] // 2, 1)
    other = 1 - half
    out_ref[...] = jnp.zeros_like(out_ref)
    for i in range(8):
        block_at(keys_ref, half_block(i, half))[...] = half_ref[i * BLOCK : (i + 1) * BLOCK]
    for k in range(4):
        block = jnp.bitwise_xor(blocks_ref[k], 2)
        part = slice(k * BLOCK, (k + 1) * BLOCK)
        block_at(keys_ref, block)[...] = core_ref[part]
        block_at(keys_ref, jnp.bitwise_xor(block, 1))[...] = far_ref[part]

    @pl.loop(0, 4)
    def _(rb):
        own_block = blocks_ref[rb]
        own = block_at(keys_ref, own_block)
        row_positions = across(own_block * BLOCK)
        _, _, _, low_block, all_blocks = docs.of_rows(own_block)
        sums[...] = part_ref[rb]

        def key_at(index):
            return block_at(keys_ref, half_block(index, other))

        add_half(docs, own_block, other, own, key_at, sums)

        fine = jnp.logical_and(jnp.max(sums[0:1]) < SUM_LIMIT, jnp.max(sums[1:2]) < SUM_LIMIT)

        @pl.when(jnp.logical_not(fine))
        def _():
            sums[...] = jnp.zeros_like(sums)
            max_t[...] = jnp.full_like(max_t, NEG_FILL)
            max_s[...] = jnp.full_like(max_s, NEG_FILL)
            row_docs = docs.of(row_positions)
            first = low_block

            @pl.loop(0, all_blocks)
            def _(j):
                t, s = scores(block_at(keys_ref, first + j)[...], own[...])
                keep = docs.of(down((first + j) * BLOCK)) == row_docs
                kept_t = jnp.where(keep, t, NEG_FILL)
                kept_s = jnp.where(keep, s, NEG_FILL)
                old_t = max_t[0:1]
                old_s = max_s[0:1]
                new_t = jnp.maximum(old_t, jnp.max(kept_t, axis=0, keepdims=True))
                new_s = jnp.maximum(old_s, jnp.max(kept_s, axis=0, keepdims=True))
                et = jnp.where(keep, jnp.exp2(kept_t - new_t), 0.0)
                es = jnp.where(keep, jnp.exp2(kept_s - new_s), 0.0)
                shrink_t = jnp.exp2(old_t - new_t)
                sums[0:1] = sums[0:1] * shrink_t + as_row(et)
                sums[1:2] = sums[1:2] * jnp.exp2(old_s - new_s) + as_row(es)
                sums[2:3] = sums[2:3] * shrink_t + as_row(et * (t - s))
                max_t[0:1] = new_t
                max_s[0:1] = new_s

        @pl.when(fine)
        def _():
            max_t[...] = jnp.zeros_like(max_t)
            max_s[...] = jnp.zeros_like(max_s)

        lse_t = jnp.log(sums[0:1]) + LN2 * max_t[0:1]
        lse_s = jnp.log(sums[1:2]) + LN2 * max_s[0:1]
        out_ref[rb, 0:1] = lse_t
        out_ref[rb, 1:2] = lse_s
        out_ref[rb, 3:4] = part_ref[rb, 3:4]
        loss_ref[pl.ds(own_block // 4, 1)] = sums[2:3] * LN2 / sums[0:1] - lse_t + lse_s


def grad_kernel(rb, lengths_ref, blocks_ref, stats_ref, keys_ref, out_ref, row_u, acc, sym):
    docs = Documents(lengths_ref)
    own_block = blocks_ref[rb]
    has_long, has_short, short_block, low_block, all_blocks = docs.of_rows(own_block)
    own = block_at(keys_ref, own_block)
    top = stats_ref[0, 0:2]
    for i in range(1, 16):
        top = jnp.maximum(top, stats_ref[i, 0:2])
    calm = jnp.max(top) <= LSE_LIMIT
    acc[...] = jnp.zeros_like(acc)

    def factors(block):
        return stats_ref[block, 3:4] * jnp.exp(-stats_ref[block, 0:2])

    def tiles(first, count, keep_of):
        mine = factors(own_block)
        row_t = both_halves(as_column(mine[0:1]))
        row_s = both_halves(as_column(mine[1:2]))
        for j in range(count):
            key = block_at(keys_ref, first + j)
            t, s = scores(own[...], key[...])
            key_u = factors(first + j)
            symmetric = jnp.exp2(s) * (row_s + key_u[1:2]) - jnp.exp2(t) * (row_t + key_u[0:1])
            keep = keep_of(j)
            if keep is not None:
                symmetric = jnp.where(keep, symmetric, 0.0)
            sym[:, j * BLOCK : (j + 1) * BLOCK] = symmetric.astype(jnp.bfloat16)
        span = pl.ds(pl.multiple_of(first * BLOCK, BLOCK), count * BLOCK)
        return dot(sym[:, : count * BLOCK], keys_ref[span, WIDE:], NN)

    @pl.when(jnp.logical_and(calm, has_long))
    def _():
        first = docs.long_block

        def keep_of(j):
            if 0 < j < LONG_TILES - 1:
                return None
            return docs.in_longest(across((first + j) * BLOCK))

        total = tiles(first, LONG_TILES, keep_of)
        acc[...] = jnp.where(docs.in_longest(down(own_block * BLOCK)), total, 0.0)

    @pl.when(jnp.logical_and(calm, has_short))
    def _():
        first = short_block
        row_docs = docs.of(down(own_block * BLOCK))

        def keep_of(j):
            return row_docs == docs.of(across((first + j) * BLOCK))

        total = tiles(first, SHORT_TILES, keep_of)
        acc[...] = jnp.where(docs.in_longest(down(own_block * BLOCK)), acc[...], total)

    @pl.when(jnp.logical_not(calm))
    def _():
        for i in range(2):
            row_u[i] = as_column(stats_ref[own_block, i : i + 1] * LOG2E)
        row_u[2] = as_column(stats_ref[own_block, 3:4])
        row_docs = docs.of(down(own_block * BLOCK))
        first = low_block

        @pl.loop(0, all_blocks)
        def _(j):
            key = block_at(keys_ref, first + j)
            t, s = scores(own[...], key[...])
            keep = row_docs == docs.of(across((first + j) * BLOCK))
            key_lse = stats_ref[first + j, 0:2] * LOG2E

            def prob(score, lse):
                return jnp.exp2(jnp.where(keep, score - lse, NEG_FILL))

            pull = both_halves(row_u[2]) * (prob(s, both_halves(row_u[1])) - prob(t, both_halves(row_u[0])))
            pull_t = stats_ref[first + j, 3:4] * (prob(s, key_lse[1:2]) - prob(t, key_lse[0:1]))
            acc[...] += dot((pull + pull_t).astype(jnp.bfloat16), key[:, WIDE:], NN)

    out_ref[...] = (acc[...] * STUDENT_SCALE).astype(out_ref.dtype)


VMEM = pl.BlockSpec(memory_space=pltpu.VMEM)
SMEM = pl.BlockSpec(memory_space=pltpu.SMEM)


def run_early(lengths, blocks, pieces):
    return pl.pallas_call(
        early_kernel,
        out_shape=(
            jax.ShapeDtypeStruct((4, 8, BLOCK), jnp.float32),
            jax.ShapeDtypeStruct((8 * BLOCK, WIDE + NARROW), jnp.bfloat16),
        ),
        in_specs=[SMEM, SMEM] + [VMEM] * 8,
        out_specs=(VMEM, VMEM),
        scratch_shapes=[pltpu.VMEM((8, BLOCK), jnp.float32)],
        compiler_params=pltpu.CompilerParams(vmem_limit_bytes=16 * MIB),
        cost_estimate=pl.CostEstimate(flops=3 * 10**9, bytes_accessed=7 * MIB, transcendentals=0),
        name="early",
    )(lengths, blocks, *pieces)


def run_stats(lengths, blocks, part, half, core, far):
    return pl.pallas_call(
        stats_kernel,
        out_shape=(
            jax.ShapeDtypeStruct((4, 8, BLOCK), jnp.float32),
            jax.ShapeDtypeStruct((4, BLOCK), jnp.float32),
            jax.ShapeDtypeStruct((16 * BLOCK, WIDE + NARROW), jnp.bfloat16),
        ),
        in_specs=[SMEM, SMEM] + [VMEM] * 4,
        out_specs=(VMEM, VMEM, VMEM),
        scratch_shapes=[pltpu.VMEM((8, BLOCK), jnp.float32)] * 3,
        compiler_params=pltpu.CompilerParams(vmem_limit_bytes=20 * MIB),
        cost_estimate=pl.CostEstimate(flops=3 * 10**9, bytes_accessed=7 * MIB, transcendentals=0),
        name="stats",
    )(lengths, blocks, part, half, core, far)


def run_grad(rb, lengths, blocks, stats, keys):
    return pl.pallas_call(
        functools.partial(grad_kernel, rb),
        out_shape=jax.ShapeDtypeStruct((BLOCK, NARROW), jnp.bfloat16),
        in_specs=[SMEM, SMEM, VMEM, VMEM],
        out_specs=VMEM,
        scratch_shapes=[
            pltpu.VMEM((3, BLOCK, 128), jnp.float32),
            pltpu.VMEM((BLOCK, NARROW), jnp.float32),
            pltpu.VMEM((BLOCK, LONG_TILES * BLOCK), jnp.bfloat16),
        ],
        compiler_params=pltpu.CompilerParams(vmem_limit_bytes=16 * MIB),
        cost_estimate=pl.CostEstimate(flops=2 * 10**9, bytes_accessed=7 * MIB, transcendentals=0),
        name="grad",
    )(lengths, blocks, stats, keys)


def after(value, *others):
    return lax.optimization_barrier((value,) + others)[0]


def in_thirds(row):
    high = lax.reduce_precision(row, 8, 7)
    middle = lax.reduce_precision(row - high, 8, 7)
    return [part.astype(jnp.bfloat16) for part in (high, middle, row - high - middle)]


def local(teacher, student, weights, lengths):
    seq = lax.axis_index("seq")
    z, x = seq // 2, seq % 2
    head = lax.axis_index("head")
    c = head % 2
    source = (z // 2) * 2 + c

    items = [ROUNDS[PLANES.index(p)] if p in PLANES else (0, 1, 2, 3) for p in range(8)]
    quarters = [lookup([items[p][k] for p in range(8)], z) for k in range(4)]
    mine = 2 * c + x
    blocks = jnp.stack([q * 4 + mine for q in quarters])

    w_tail = jnp.concatenate(in_thirds(weights.reshape(1, BLOCK)), axis=1)
    w_tail = jnp.pad(w_tail, ((0, 15), (0, 0)))

    def message(k):
        sent = [relation_sent(k, q, core) or 0 for q in range(4) for core in range(2)]
        r = lookup(sent, source)
        vectors = [lax.dynamic_index_in_dim(v, r, 0, False) for v in (teacher, student)]
        return jnp.concatenate([jnp.concatenate(vectors, axis=1), w_tail], axis=0)

    own = [permute(message(k), out_pairs(k)) for k in range(4)]
    mine_only = [v[:BLOCK] for v in own]
    side = [permute(v, swap_pairs(1, 0)) for v in mine_only]
    core = permute(after(jnp.concatenate(mine_only, axis=0), side[1]), swap_pairs(0, 1))
    far = permute(jnp.concatenate(side, axis=0), swap_pairs(0, 1))
    part, half = run_early(lengths, blocks, own + side)
    stats, loss, keys = run_stats(lengths, blocks, part, half, core, far)

    both = jnp.stack([stats, permute(stats, swap_pairs(1, 0))])
    four = [both, permute(both, swap_pairs(0, 1))]
    all_stats = jnp.zeros((16, 8, BLOCK), jnp.float32)
    for flip in range(4):
        for k in range(4):
            where = quarters[k] * 4 + (mine ^ flip)
            all_stats = lax.dynamic_update_slice(
                all_stats, four[flip // 2][flip % 2, k : k + 1], (where, 0, 0)
            )
    grads = []
    for step, (dz, dh) in enumerate(((0, 2), (0, 4), (0, 8), (4, 0))):
        pairs = [(place(z, x, g, c), place(z ^ dz, x, g, c) ^ dh) for z, x, g, c in DEVICES]
        if step == 1:
            loss = after(loss, all_stats)
        elif step > 1:
            loss = after(loss, grads[step - 2])
        came = permute(loss, pairs)
        if step > 0:
            grads.append(run_grad(step - 1, lengths, blocks, all_stats, keys))
        loss = loss + came
        blocks = after(blocks, loss)
    grads.append(run_grad(3, lengths, blocks, all_stats, keys))

    back = []
    for k in range(4):
        tail = jnp.concatenate(in_thirds(lax.dynamic_slice_in_dim(loss, quarters[k], 1, 0)), axis=0)
        tail = jnp.pad(tail, ((0, 13), (0, 0)))
        back.append(permute(jnp.concatenate([grads[k], tail], axis=0), back_pairs(k)))
    total = sum(v[BLOCK : BLOCK + 3].astype(jnp.float32) for v in back)
    row_loss = jnp.sum(total, axis=0)

    back = jnp.stack([v[:BLOCK] for v in back])
    came = []
    for r in range(3):
        table = [ROUNDS[core * 3 + r].index(q) for q in range(4) for core in range(2)]
        came.append(lax.dynamic_index_in_dim(back, lookup(table, source), 0, False))
    return (row_loss, jnp.stack(came).astype(jnp.float32))


def solution(mesh):
    return jax.shard_map(
        local,
        mesh=mesh,
        in_specs=(P(None, "seq", "head"), P(None, "seq", "head"), P("seq"), P()),
        out_specs=(P("seq"), P(None, "seq", "head")),
        check_vma=False,
    )
```

```python
import functools
import math

import jax
import jax.numpy as jnp
from jax import lax
from jax.experimental import pallas as pl
from jax.experimental.pallas import tpu as pltpu
from jax.sharding import PartitionSpec as P

AXES = ("seq", "head")
PLANES = (0, 1, 2, 4, 5, 6)
ROUNDS = ((0, 1, 2, 3), (3, 2, 1, 0), (1, 3, 0, 2), (1, 3, 0, 2), (0, 2, 1, 3), (3, 1, 2, 0))
BLOCK = 256
WIDE = 512
NARROW = 256
LOG2E = math.log2(math.e)
LN2 = math.log(2.0)
TEACHER_SCALE = 1.0 / math.sqrt(WIDE)
STUDENT_SCALE = 1.0 / math.sqrt(NARROW)
NEG_FILL = -1e30
SUM_LIMIT = 1e30
LSE_LIMIT = 60.0
MIB = 1 << 20


def place(z, x, g, c):
    return (z * 2 + x) * 16 + g * 2 + c


DEVICES = [(z, x, g, c) for z in range(8) for x in range(2) for g in range(8) for c in range(2)]


def relation_sent(k, quarter, core):
    for r in range(3):
        if ROUNDS[core * 3 + r][k] == quarter:
            return r
    return None


def out_pairs(k):
    pairs = []
    for z, x, g, c in DEVICES:
        r = relation_sent(k, z // 2, c)
        if r is not None:
            pairs.append((place(z, x, g, c), place(PLANES[c * 3 + r], x, g, z % 2)))
    return pairs


def lookup(table, index):
    code = sum(int(value) << (2 * i) for i, value in enumerate(table))
    return lax.shift_right_logical(jnp.int32(code), (2 * index).astype(jnp.int32)) & 3


def back_pairs(k):
    return [(b, a) for a, b in out_pairs(k)]


def swap_pairs(dx, dc):
    return [(place(z, x, g, c), place(z, x ^ dx, g, c ^ dc)) for z, x, g, c in DEVICES if z in PLANES]


def permute(value, pairs):
    return lax.ppermute(value, AXES, pairs)


NT = (((1,), (1,)), ((), ()))
NN = (((1,), (0,)), ((), ()))


def dot(a, b, dims):
    return lax.dot_general(a, b, dims, preferred_element_type=jnp.float32)


def scores(rows, keys):
    t = dot(rows[:, :WIDE], keys[:, :WIDE], NT) * (TEACHER_SCALE * LOG2E)
    s = dot(rows[:, WIDE:], keys[:, WIDE:], NT) * (STUDENT_SCALE * LOG2E)
    return t, s


class Documents:
    def __init__(self, lengths_ref):
        self.starts, self.ends = [], []
        end = jnp.int32(0)
        for d in range(4):
            self.starts.append(end)
            end = end + lengths_ref[d]
            self.ends.append(end)
        self.long_start, self.long_end = self.starts[0], self.ends[0]
        for d in range(1, 4):
            longer = self.ends[d] - self.starts[d] > self.long_end - self.long_start
            self.long_start = jnp.where(longer, self.starts[d], self.long_start)
            self.long_end = jnp.where(longer, self.ends[d], self.long_end)
        self.long_block = jnp.minimum(self.long_start // BLOCK, 16 - LONG_TILES)

    def of(self, positions):
        total = jnp.zeros(positions.shape, jnp.int32)
        for end in self.ends:
            total += jnp.where(positions >= end, 1, 0)
        return total

    def in_longest(self, positions):
        return jnp.logical_and(positions >= self.long_start, positions < self.long_end)

    def of_rows(self, block):
        first = block * BLOCK
        last = first + (BLOCK - 1)
        low, high = jnp.int32(0), jnp.int32(16 * BLOCK)
        for start, end in zip(self.starts, self.ends):
            low = jnp.maximum(low, jnp.where(start <= first, start, 0))
            high = jnp.minimum(high, jnp.where(end > last, end, 16 * BLOCK))
        has_long = jnp.logical_and(last >= self.long_start, first < self.long_end)
        short_low = jnp.where(low == self.long_start, self.long_end, low)
        short_high = jnp.where(high == self.long_end, self.long_start, high)
        has_short = short_high > short_low
        short_block = jnp.minimum(short_low // BLOCK, 16 - SHORT_TILES)
        block_low = low // BLOCK
        return has_long, has_short, short_block, block_low, (high + BLOCK - 1) // BLOCK - block_low


def down(base):
    return base + lax.broadcasted_iota(jnp.int32, (BLOCK, 1), 0)


def across(base):
    return base + lax.broadcasted_iota(jnp.int32, (1, BLOCK), 1)


def fold(v):
    return jnp.sum(v.reshape(BLOCK // 8, 8, BLOCK), axis=0)


def as_row(v):
    return jnp.sum(v, axis=0, keepdims=True)


def as_column(row):
    return jnp.broadcast_to(row, (128, BLOCK)).T


def both_halves(v):
    return jnp.concatenate([v, v], axis=1)


def block_at(ref, index):
    return ref.at[pl.ds(pl.multiple_of(index * BLOCK, BLOCK), BLOCK)]


LONG_TILES = 13
SHORT_TILES = 5
LONG_HALF = 7
SHORT_HALF = 3


def half_block(index, half):
    return (index // 2) * 4 + 2 * half + index % 2


def half_window(first, half, count):
    inside = jnp.bitwise_and(first // 2, 1) == half
    low = jnp.where(inside, first % 2, jnp.where(half == 1, 0, 2))
    return jnp.minimum((first // 4) * 2 + low, 8 - count)


def add_half(docs, own_block, half, own, key_at, sums):
    row_positions = across(own_block * BLOCK)
    has_long, has_short, short_block, _, _ = docs.of_rows(own_block)

    def tiles(first, count, keep_of):
        part_t = jnp.zeros((8, BLOCK), jnp.float32)
        part_c = jnp.zeros((8, BLOCK), jnp.float32)
        part_s = jnp.zeros((8, BLOCK), jnp.float32)
        for j in range(count):
            t, s = scores(key_at(first + j)[...], own[...])
            et = jnp.exp2(t)
            es = jnp.exp2(s)
            keep = keep_of(j, down(half_block(first + j, half) * BLOCK))
            if keep is not None:
                et = jnp.where(keep, et, 0.0)
                es = jnp.where(keep, es, 0.0)
            part_t += fold(et)
            part_s += fold(es)
            part_c += fold(et * (t - s))
        return as_row(part_t), as_row(part_s), as_row(part_c)

    def add(parts, rows):
        for i, part in enumerate(parts):
            sums[i : i + 1] += jnp.where(rows, part, 0.0)

    @pl.when(has_long)
    def _():
        first = half_window(docs.long_start // BLOCK, half, LONG_HALF)

        def keep_of(j, positions):
            return None if 0 < j < LONG_HALF - 1 else docs.in_longest(positions)

        add(tiles(first, LONG_HALF, keep_of), docs.in_longest(row_positions))

    @pl.when(has_short)
    def _():
        first = half_window(short_block, half, SHORT_HALF)
        row_docs = docs.of(row_positions)

        def keep_of(j, positions):
            return docs.of(positions) == row_docs

        add(tiles(first, SHORT_HALF, keep_of), jnp.logical_not(docs.in_longest(row_positions)))


def early_kernel(lengths_ref, blocks_ref, *refs):
    own_refs, side_refs, out_ref, half_ref, sums = refs[:4], refs[4:8], refs[8], refs[9], refs[10]
    docs = Documents(lengths_ref)
    half = jnp.bitwise_and(blocks_ref[0] // 2, 1)
    out_ref[...] = jnp.zeros_like(out_ref)
    for k in range(4):
        index = (blocks_ref[k] // 4) * 2 + blocks_ref[k] % 2
        block_at(half_ref, index)[...] = own_refs[k][:BLOCK]
        block_at(half_ref, jnp.bitwise_xor(index, 1))[...] = side_refs[k][...]
        tail = own_refs[k][BLOCK:].astype(jnp.float32)
        out_ref[k, 3:4] = tail[:1, :BLOCK] + tail[:1, BLOCK : 2 * BLOCK] + tail[:1, 2 * BLOCK :]

    @pl.loop(0, 4)
    def _(rb):
        own_block = blocks_ref[rb]
        sums[...] = jnp.zeros_like(sums)
        own = block_at(half_ref, (own_block // 4) * 2 + own_block % 2)
        add_half(docs, own_block, half, own, functools.partial(block_at, half_ref), sums)
        out_ref[rb, 0:3] = sums[0:3]


def stats_kernel(lengths_ref, blocks_ref, part_ref, half_ref, core_ref, far_ref, *refs):
    out_ref, loss_ref, keys_ref, sums, max_t, max_s = refs
    docs = Documents(lengths_ref)
    half = jnp.bitwise_and(blocks_ref[0] // 2, 1)
    other = 1 - half
    out_ref[...] = jnp.zeros_like(out_ref)
    for i in range(8):
        block_at(keys_ref, half_block(i, half))[...] = half_ref[i * BLOCK : (i + 1) * BLOCK]
    for k in range(4):
        block = jnp.bitwise_xor(blocks_ref[k], 2)
        part = slice(k * BLOCK, (k + 1) * BLOCK)
        block_at(keys_ref, block)[...] = core_ref[part]
        block_at(keys_ref, jnp.bitwise_xor(block, 1))[...] = far_ref[part]

    @pl.loop(0, 4)
    def _(rb):
        own_block = blocks_ref[rb]
        own = block_at(keys_ref, own_block)
        row_positions = across(own_block * BLOCK)
        _, _, _, low_block, all_blocks = docs.of_rows(own_block)
        sums[...] = part_ref[rb]

        def key_at(index):
            return block_at(keys_ref, half_block(index, other))

        add_half(docs, own_block, other, own, key_at, sums)

        fine = jnp.logical_and(jnp.max(sums[0:1]) < SUM_LIMIT, jnp.max(sums[1:2]) < SUM_LIMIT)

        @pl.when(jnp.logical_not(fine))
        def _():
            sums[...] = jnp.zeros_like(sums)
            max_t[...] = jnp.full_like(max_t, NEG_FILL)
            max_s[...] = jnp.full_like(max_s, NEG_FILL)
            row_docs = docs.of(row_positions)
            first = low_block

            @pl.loop(0, all_blocks)
            def _(j):
                t, s = scores(block_at(keys_ref, first + j)[...], own[...])
                keep = docs.of(down((first + j) * BLOCK)) == row_docs
                kept_t = jnp.where(keep, t, NEG_FILL)
                kept_s = jnp.where(keep, s, NEG_FILL)
                old_t = max_t[0:1]
                old_s = max_s[0:1]
                new_t = jnp.maximum(old_t, jnp.max(kept_t, axis=0, keepdims=True))
                new_s = jnp.maximum(old_s, jnp.max(kept_s, axis=0, keepdims=True))
                et = jnp.where(keep, jnp.exp2(kept_t - new_t), 0.0)
                es = jnp.where(keep, jnp.exp2(kept_s - new_s), 0.0)
                shrink_t = jnp.exp2(old_t - new_t)
                sums[0:1] = sums[0:1] * shrink_t + as_row(et)
                sums[1:2] = sums[1:2] * jnp.exp2(old_s - new_s) + as_row(es)
                sums[2:3] = sums[2:3] * shrink_t + as_row(et * (t - s))
                max_t[0:1] = new_t
                max_s[0:1] = new_s

        @pl.when(fine)
        def _():
            max_t[...] = jnp.zeros_like(max_t)
            max_s[...] = jnp.zeros_like(max_s)

        lse_t = jnp.log(sums[0:1]) + LN2 * max_t[0:1]
        lse_s = jnp.log(sums[1:2]) + LN2 * max_s[0:1]
        out_ref[rb, 0:1] = lse_t
        out_ref[rb, 1:2] = lse_s
        out_ref[rb, 3:4] = part_ref[rb, 3:4]
        loss_ref[pl.ds(own_block // 4, 1)] = sums[2:3] * LN2 / sums[0:1] - lse_t + lse_s


def grad_kernel(rb, lengths_ref, blocks_ref, stats_ref, keys_ref, out_ref, row_u, acc, sym):
    docs = Documents(lengths_ref)
    own_block = blocks_ref[rb]
    has_long, has_short, short_block, low_block, all_blocks = docs.of_rows(own_block)
    own = block_at(keys_ref, own_block)
    top = stats_ref[0, 0:2]
    for i in range(1, 16):
        top = jnp.maximum(top, stats_ref[i, 0:2])
    calm = jnp.max(top) <= LSE_LIMIT
    acc[...] = jnp.zeros_like(acc)

    def factors(block):
        return stats_ref[block, 3:4] * jnp.exp(-stats_ref[block, 0:2])

    def tiles(first, count, keep_of):
        mine = factors(own_block)
        row_t = both_halves(as_column(mine[0:1]))
        row_s = both_halves(as_column(mine[1:2]))
        for j in range(count):
            key = block_at(keys_ref, first + j)
            t, s = scores(own[...], key[...])
            key_u = factors(first + j)
            symmetric = jnp.exp2(s) * (row_s + key_u[1:2]) - jnp.exp2(t) * (row_t + key_u[0:1])
            keep = keep_of(j)
            if keep is not None:
                symmetric = jnp.where(keep, symmetric, 0.0)
            sym[:, j * BLOCK : (j + 1) * BLOCK] = symmetric.astype(jnp.bfloat16)
        span = pl.ds(pl.multiple_of(first * BLOCK, BLOCK), count * BLOCK)
        return dot(sym[:, : count * BLOCK], keys_ref[span, WIDE:], NN)

    @pl.when(jnp.logical_and(calm, has_long))
    def _():
        first = docs.long_block

        def keep_of(j):
            if 0 < j < LONG_TILES - 1:
                return None
            return docs.in_longest(across((first + j) * BLOCK))

        total = tiles(first, LONG_TILES, keep_of)
        acc[...] = jnp.where(docs.in_longest(down(own_block * BLOCK)), total, 0.0)

    @pl.when(jnp.logical_and(calm, has_short))
    def _():
        first = short_block
        row_docs = docs.of(down(own_block * BLOCK))

        def keep_of(j):
            return row_docs == docs.of(across((first + j) * BLOCK))

        total = tiles(first, SHORT_TILES, keep_of)
        acc[...] = jnp.where(docs.in_longest(down(own_block * BLOCK)), acc[...], total)

    @pl.when(jnp.logical_not(calm))
    def _():
        for i in range(2):
            row_u[i] = as_column(stats_ref[own_block, i : i + 1] * LOG2E)
        row_u[2] = as_column(stats_ref[own_block, 3:4])
        row_docs = docs.of(down(own_block * BLOCK))
        first = low_block

        @pl.loop(0, all_blocks)
        def _(j):
            key = block_at(keys_ref, first + j)
            t, s = scores(own[...], key[...])
            keep = row_docs == docs.of(across((first + j) * BLOCK))
            key_lse = stats_ref[first + j, 0:2] * LOG2E

            def prob(score, lse):
                return jnp.exp2(jnp.where(keep, score - lse, NEG_FILL))

            pull = both_halves(row_u[2]) * (prob(s, both_halves(row_u[1])) - prob(t, both_halves(row_u[0])))
            pull_t = stats_ref[first + j, 3:4] * (prob(s, key_lse[1:2]) - prob(t, key_lse[0:1]))
            acc[...] += dot((pull + pull_t).astype(jnp.bfloat16), key[:, WIDE:], NN)

    out_ref[...] = (acc[...] * STUDENT_SCALE).astype(out_ref.dtype)


VMEM = pl.BlockSpec(memory_space=pltpu.VMEM)
SMEM = pl.BlockSpec(memory_space=pltpu.SMEM)


def run_early(lengths, blocks, pieces):
    return pl.pallas_call(
        early_kernel,
        out_shape=(
            jax.ShapeDtypeStruct((4, 8, BLOCK), jnp.float32),
            jax.ShapeDtypeStruct((8 * BLOCK, WIDE + NARROW), jnp.bfloat16),
        ),
        in_specs=[SMEM, SMEM] + [VMEM] * 8,
        out_specs=(VMEM, VMEM),
        scratch_shapes=[pltpu.VMEM((8, BLOCK), jnp.float32)],
        compiler_params=pltpu.CompilerParams(vmem_limit_bytes=16 * MIB),
        cost_estimate=pl.CostEstimate(flops=3 * 10**9, bytes_accessed=7 * MIB, transcendentals=0),
        name="early",
    )(lengths, blocks, *pieces)


def run_stats(lengths, blocks, part, half, core, far):
    return pl.pallas_call(
        stats_kernel,
        out_shape=(
            jax.ShapeDtypeStruct((4, 8, BLOCK), jnp.float32),
            jax.ShapeDtypeStruct((4, BLOCK), jnp.float32),
            jax.ShapeDtypeStruct((16 * BLOCK, WIDE + NARROW), jnp.bfloat16),
        ),
        in_specs=[SMEM, SMEM] + [VMEM] * 4,
        out_specs=(VMEM, VMEM, VMEM),
        scratch_shapes=[pltpu.VMEM((8, BLOCK), jnp.float32)] * 3,
        compiler_params=pltpu.CompilerParams(vmem_limit_bytes=20 * MIB),
        cost_estimate=pl.CostEstimate(flops=3 * 10**9, bytes_accessed=7 * MIB, transcendentals=0),
        name="stats",
    )(lengths, blocks, part, half, core, far)


def run_grad(rb, lengths, blocks, stats, keys):
    return pl.pallas_call(
        functools.partial(grad_kernel, rb),
        out_shape=jax.ShapeDtypeStruct((BLOCK, NARROW), jnp.bfloat16),
        in_specs=[SMEM, SMEM, VMEM, VMEM],
        out_specs=VMEM,
        scratch_shapes=[
            pltpu.VMEM((3, BLOCK, 128), jnp.float32),
            pltpu.VMEM((BLOCK, NARROW), jnp.float32),
            pltpu.VMEM((BLOCK, LONG_TILES * BLOCK), jnp.bfloat16),
        ],
        compiler_params=pltpu.CompilerParams(vmem_limit_bytes=16 * MIB),
        cost_estimate=pl.CostEstimate(flops=2 * 10**9, bytes_accessed=7 * MIB, transcendentals=0),
        name="grad",
    )(lengths, blocks, stats, keys)


def after(value, *others):
    return lax.optimization_barrier((value,) + others)[0]


def in_thirds(row):
    high = lax.reduce_precision(row, 8, 7)
    middle = lax.reduce_precision(row - high, 8, 7)
    return [part.astype(jnp.bfloat16) for part in (high, middle, row - high - middle)]


def local(teacher, student, weights, lengths):
    seq = lax.axis_index("seq")
    z, x = seq // 2, seq % 2
    head = lax.axis_index("head")
    c = head % 2
    source = (z // 2) * 2 + c

    items = [ROUNDS[PLANES.index(p)] if p in PLANES else (0, 1, 2, 3) for p in range(8)]
    quarters = [lookup([items[p][k] for p in range(8)], z) for k in range(4)]
    mine = 2 * c + x
    blocks = jnp.stack([q * 4 + mine for q in quarters])

    w_tail = jnp.concatenate(in_thirds(weights.reshape(1, BLOCK)), axis=1)
    w_tail = jnp.pad(w_tail, ((0, 15), (0, 0)))

    def message(k):
        sent = [relation_sent(k, q, core) or 0 for q in range(4) for core in range(2)]
        r = lookup(sent, source)
        vectors = [lax.dynamic_index_in_dim(v, r, 0, False) for v in (teacher, student)]
        return jnp.concatenate([jnp.concatenate(vectors, axis=1), w_tail], axis=0)

    own = [permute(message(k), out_pairs(k)) for k in range(4)]
    mine_only = [v[:BLOCK] for v in own]
    side = [permute(v, swap_pairs(1, 0)) for v in mine_only]
    core = permute(after(jnp.concatenate(mine_only, axis=0), side[1]), swap_pairs(0, 1))
    far = permute(jnp.concatenate(side, axis=0), swap_pairs(0, 1))
    part, half = run_early(lengths, blocks, own + side)
    stats, loss, keys = run_stats(lengths, blocks, part, half, core, far)

    both = jnp.stack([stats, permute(stats, swap_pairs(1, 0))])
    four = [both, permute(both, swap_pairs(0, 1))]
    all_stats = jnp.zeros((16, 8, BLOCK), jnp.float32)
    for flip in range(4):
        for k in range(4):
            where = quarters[k] * 4 + (mine ^ flip)
            all_stats = lax.dynamic_update_slice(
                all_stats, four[flip // 2][flip % 2, k : k + 1], (where, 0, 0)
            )
    grads = []
    for step, dh in enumerate((2, 4, 8)):
        loss = after(loss, all_stats if step == 0 else grads[step - 1])
        came = permute(loss, [(place(z, x, g, c), place(z, x, g, c) ^ dh) for z, x, g, c in DEVICES])
        grads.append(run_grad(step, lengths, blocks, all_stats, keys))
        loss = loss + came
        blocks = after(blocks, loss)
    grads.append(run_grad(3, lengths, blocks, all_stats, keys))

    back = []
    for k in range(4):
        tail = jnp.concatenate(in_thirds(lax.dynamic_slice_in_dim(loss, quarters[k], 1, 0)), axis=0)
        tail = jnp.pad(tail, ((0, 13), (0, 0)))
        back.append(permute(jnp.concatenate([grads[k], tail], axis=0), back_pairs(k)))
    total = sum(v[BLOCK : BLOCK + 3].astype(jnp.float32) for v in back)
    total = jnp.sum(total, axis=0, keepdims=True)
    total = total + permute(
        total, [(place(z, x, g, c), place(z, x, g, c) ^ 1) for z, x, g, c in DEVICES]
    )
    row_loss = total.reshape(BLOCK)

    back = jnp.stack([v[:BLOCK] for v in back])
    came = []
    for r in range(3):
        table = [ROUNDS[core * 3 + r].index(q) for q in range(4) for core in range(2)]
        came.append(lax.dynamic_index_in_dim(back, lookup(table, source), 0, False))
    return (row_loss, jnp.stack(came).astype(jnp.float32))


def solution(mesh):
    return jax.shard_map(
        local,
        mesh=mesh,
        in_specs=(P(None, "seq", "head"), P(None, "seq", "head"), P("seq"), P()),
        out_specs=(P("seq"), P(None, "seq", "head")),
        check_vma=False,
    )
```

```python
import functools
import math

import jax
import jax.numpy as jnp
from jax import lax
from jax.experimental import pallas as pl
from jax.experimental.pallas import tpu as pltpu
from jax.sharding import PartitionSpec as P

AXES = ("seq", "head")
PLANES = (0, 1, 2, 4, 5, 6)
ROUNDS = ((0, 1, 2, 3), (3, 2, 1, 0), (1, 3, 0, 2), (1, 3, 0, 2), (0, 2, 1, 3), (3, 1, 2, 0))
BLOCK = 256
WIDE = 512
NARROW = 256
LOG2E = math.log2(math.e)
LN2 = math.log(2.0)
TEACHER_SCALE = 1.0 / math.sqrt(WIDE)
STUDENT_SCALE = 1.0 / math.sqrt(NARROW)
NEG_FILL = -1e30
SUM_LIMIT = 1e30
LSE_LIMIT = 60.0
MIB = 1 << 20


def place(z, x, g, c):
    return (z * 2 + x) * 16 + g * 2 + c


DEVICES = [(z, x, g, c) for z in range(8) for x in range(2) for g in range(8) for c in range(2)]


def relation_sent(k, quarter, core):
    for r in range(3):
        if ROUNDS[core * 3 + r][k] == quarter:
            return r
    return None


def out_pairs(k):
    pairs = []
    for z, x, g, c in DEVICES:
        r = relation_sent(k, z // 2, c)
        if r is not None:
            pairs.append((place(z, x, g, c), place(PLANES[c * 3 + r], x, g, z % 2)))
    return pairs


def lookup(table, index):
    code = sum(int(value) << (2 * i) for i, value in enumerate(table))
    return lax.shift_right_logical(jnp.int32(code), (2 * index).astype(jnp.int32)) & 3


def back_pairs(k):
    return [(b, a) for a, b in out_pairs(k)]


def swap_pairs(dx, dc):
    return [(place(z, x, g, c), place(z, x ^ dx, g, c ^ dc)) for z, x, g, c in DEVICES if z in PLANES]


def permute(value, pairs):
    return lax.ppermute(value, AXES, pairs)


NT = (((1,), (1,)), ((), ()))
NN = (((1,), (0,)), ((), ()))


def dot(a, b, dims):
    return lax.dot_general(a, b, dims, preferred_element_type=jnp.float32)


def scores(rows, keys):
    t = dot(rows[:, :WIDE], keys[:, :WIDE], NT) * (TEACHER_SCALE * LOG2E)
    s = dot(rows[:, WIDE:], keys[:, WIDE:], NT) * (STUDENT_SCALE * LOG2E)
    return t, s


class Documents:
    def __init__(self, lengths_ref):
        self.starts, self.ends = [], []
        end = jnp.int32(0)
        for d in range(4):
            self.starts.append(end)
            end = end + lengths_ref[d]
            self.ends.append(end)
        self.long_start, self.long_end = self.starts[0], self.ends[0]
        for d in range(1, 4):
            longer = self.ends[d] - self.starts[d] > self.long_end - self.long_start
            self.long_start = jnp.where(longer, self.starts[d], self.long_start)
            self.long_end = jnp.where(longer, self.ends[d], self.long_end)
        self.long_block = jnp.minimum(self.long_start // BLOCK, 16 - LONG_TILES)

    def of(self, positions):
        total = jnp.zeros(positions.shape, jnp.int32)
        for end in self.ends:
            total += jnp.where(positions >= end, 1, 0)
        return total

    def in_longest(self, positions):
        return jnp.logical_and(positions >= self.long_start, positions < self.long_end)

    def of_rows(self, block):
        first = block * BLOCK
        last = first + (BLOCK - 1)
        low, high = jnp.int32(0), jnp.int32(16 * BLOCK)
        for start, end in zip(self.starts, self.ends):
            low = jnp.maximum(low, jnp.where(start <= first, start, 0))
            high = jnp.minimum(high, jnp.where(end > last, end, 16 * BLOCK))
        has_long = jnp.logical_and(last >= self.long_start, first < self.long_end)
        short_low = jnp.where(low == self.long_start, self.long_end, low)
        short_high = jnp.where(high == self.long_end, self.long_start, high)
        has_short = short_high > short_low
        short_block = jnp.minimum(short_low // BLOCK, 16 - SHORT_TILES)
        block_low = low // BLOCK
        return has_long, has_short, short_block, block_low, (high + BLOCK - 1) // BLOCK - block_low


def down(base):
    return base + lax.broadcasted_iota(jnp.int32, (BLOCK, 1), 0)


def across(base):
    return base + lax.broadcasted_iota(jnp.int32, (1, BLOCK), 1)


def fold(v):
    return jnp.sum(v.reshape(BLOCK // 8, 8, BLOCK), axis=0)


def as_row(v):
    return jnp.sum(v, axis=0, keepdims=True)


def as_column(row):
    return jnp.broadcast_to(row, (128, BLOCK)).T


def both_halves(v):
    return jnp.concatenate([v, v], axis=1)


def block_at(ref, index):
    return ref.at[pl.ds(pl.multiple_of(index * BLOCK, BLOCK), BLOCK)]


LONG_TILES = 13
SHORT_TILES = 5
LONG_HALF = 7
SHORT_HALF = 3


def half_block(index, half):
    return (index // 2) * 4 + 2 * half + index % 2


def half_window(first, half, count):
    inside = jnp.bitwise_and(first // 2, 1) == half
    low = jnp.where(inside, first % 2, jnp.where(half == 1, 0, 2))
    return jnp.minimum((first // 4) * 2 + low, 8 - count)


def add_half(docs, own_block, half, own, key_at, sums):
    row_positions = across(own_block * BLOCK)
    has_long, has_short, short_block, _, _ = docs.of_rows(own_block)

    def tiles(first, count, keep_of):
        part_t = jnp.zeros((8, BLOCK), jnp.float32)
        part_c = jnp.zeros((8, BLOCK), jnp.float32)
        part_s = jnp.zeros((8, BLOCK), jnp.float32)
        for j in range(count):
            t, s = scores(key_at(first + j)[...], own[...])
            et = jnp.exp2(t)
            es = jnp.exp2(s)
            keep = keep_of(j, down(half_block(first + j, half) * BLOCK))
            if keep is not None:
                et = jnp.where(keep, et, 0.0)
                es = jnp.where(keep, es, 0.0)
            part_t += fold(et)
            part_s += fold(es)
            part_c += fold(et * (t - s))
        return as_row(part_t), as_row(part_s), as_row(part_c)

    def add(parts, rows):
        for i, part in enumerate(parts):
            sums[i : i + 1] += jnp.where(rows, part, 0.0)

    @pl.when(has_long)
    def _():
        first = half_window(docs.long_start // BLOCK, half, LONG_HALF)

        def keep_of(j, positions):
            return None if 0 < j < LONG_HALF - 1 else docs.in_longest(positions)

        add(tiles(first, LONG_HALF, keep_of), docs.in_longest(row_positions))

    @pl.when(has_short)
    def _():
        first = half_window(short_block, half, SHORT_HALF)
        row_docs = docs.of(row_positions)

        def keep_of(j, positions):
            return docs.of(positions) == row_docs

        add(tiles(first, SHORT_HALF, keep_of), jnp.logical_not(docs.in_longest(row_positions)))


def early_kernel(lengths_ref, blocks_ref, *refs):
    own_refs, side_refs, out_ref, half_ref, sums = refs[:4], refs[4:8], refs[8], refs[9], refs[10]
    docs = Documents(lengths_ref)
    half = jnp.bitwise_and(blocks_ref[0] // 2, 1)
    out_ref[...] = jnp.zeros_like(out_ref)
    for k in range(4):
        index = (blocks_ref[k] // 4) * 2 + blocks_ref[k] % 2
        block_at(half_ref, index)[...] = own_refs[k][:BLOCK]
        block_at(half_ref, jnp.bitwise_xor(index, 1))[...] = side_refs[k][...]
        tail = own_refs[k][BLOCK:].astype(jnp.float32)
        out_ref[k, 3:4] = tail[:1, :BLOCK] + tail[:1, BLOCK : 2 * BLOCK] + tail[:1, 2 * BLOCK :]

    @pl.loop(0, 4)
    def _(rb):
        own_block = blocks_ref[rb]
        sums[...] = jnp.zeros_like(sums)
        own = block_at(half_ref, (own_block // 4) * 2 + own_block % 2)
        add_half(docs, own_block, half, own, functools.partial(block_at, half_ref), sums)
        out_ref[rb, 0:3] = sums[0:3]


def stats_kernel(lengths_ref, blocks_ref, part_ref, half_ref, core_ref, far_ref, *refs):
    out_ref, loss_ref, keys_ref, sums, max_t, max_s, arrived = refs
    docs = Documents(lengths_ref)
    half = jnp.bitwise_and(blocks_ref[0] // 2, 1)
    other = 1 - half
    out_ref[...] = jnp.zeros_like(out_ref)
    copies = []
    for k in range(4):
        block = jnp.bitwise_xor(blocks_ref[k], 2)
        part = pl.ds(k * BLOCK, BLOCK)
        for i, (source, target) in enumerate(((core_ref, block), (far_ref, jnp.bitwise_xor(block, 1)))):
            copies.append(
                pltpu.make_async_copy(source.at[part], block_at(keys_ref, target), arrived.at[2 * k + i])
            )
            copies[-1].start()
    for i in range(8):
        block_at(keys_ref, half_block(i, half))[...] = half_ref[i * BLOCK : (i + 1) * BLOCK]
    for copy in copies:
        copy.wait()

    @pl.loop(0, 4)
    def _(rb):
        own_block = blocks_ref[rb]
        own = block_at(keys_ref, own_block)
        row_positions = across(own_block * BLOCK)
        _, _, _, low_block, all_blocks = docs.of_rows(own_block)
        sums[...] = part_ref[rb]

        def key_at(index):
            return block_at(keys_ref, half_block(index, other))

        add_half(docs, own_block, other, own, key_at, sums)

        fine = jnp.logical_and(jnp.max(sums[0:1]) < SUM_LIMIT, jnp.max(sums[1:2]) < SUM_LIMIT)

        @pl.when(jnp.logical_not(fine))
        def _():
            sums[...] = jnp.zeros_like(sums)
            max_t[...] = jnp.full_like(max_t, NEG_FILL)
            max_s[...] = jnp.full_like(max_s, NEG_FILL)
            row_docs = docs.of(row_positions)
            first = low_block

            @pl.loop(0, all_blocks)
            def _(j):
                t, s = scores(block_at(keys_ref, first + j)[...], own[...])
                keep = docs.of(down((first + j) * BLOCK)) == row_docs
                kept_t = jnp.where(keep, t, NEG_FILL)
                kept_s = jnp.where(keep, s, NEG_FILL)
                old_t = max_t[0:1]
                old_s = max_s[0:1]
                new_t = jnp.maximum(old_t, jnp.max(kept_t, axis=0, keepdims=True))
                new_s = jnp.maximum(old_s, jnp.max(kept_s, axis=0, keepdims=True))
                et = jnp.where(keep, jnp.exp2(kept_t - new_t), 0.0)
                es = jnp.where(keep, jnp.exp2(kept_s - new_s), 0.0)
                shrink_t = jnp.exp2(old_t - new_t)
                sums[0:1] = sums[0:1] * shrink_t + as_row(et)
                sums[1:2] = sums[1:2] * jnp.exp2(old_s - new_s) + as_row(es)
                sums[2:3] = sums[2:3] * shrink_t + as_row(et * (t - s))
                max_t[0:1] = new_t
                max_s[0:1] = new_s

        @pl.when(fine)
        def _():
            max_t[...] = jnp.zeros_like(max_t)
            max_s[...] = jnp.zeros_like(max_s)

        lse_t = jnp.log(sums[0:1]) + LN2 * max_t[0:1]
        lse_s = jnp.log(sums[1:2]) + LN2 * max_s[0:1]
        out_ref[rb, 0:1] = lse_t
        out_ref[rb, 1:2] = lse_s
        out_ref[rb, 3:4] = part_ref[rb, 3:4]
        loss_ref[pl.ds(own_block // 4, 1)] = sums[2:3] * LN2 / sums[0:1] - lse_t + lse_s


def grad_kernel(rb, lengths_ref, blocks_ref, stats_ref, keys_ref, out_ref, row_u, acc, sym):
    docs = Documents(lengths_ref)
    own_block = blocks_ref[rb]
    has_long, has_short, short_block, low_block, all_blocks = docs.of_rows(own_block)
    own = block_at(keys_ref, own_block)
    top = stats_ref[0, 0:2]
    for i in range(1, 16):
        top = jnp.maximum(top, stats_ref[i, 0:2])
    calm = jnp.max(top) <= LSE_LIMIT
    acc[...] = jnp.zeros_like(acc)

    def factors(block):
        return stats_ref[block, 3:4] * jnp.exp(-stats_ref[block, 0:2])

    def tiles(first, count, keep_of):
        mine = factors(own_block)
        row_t = both_halves(as_column(mine[0:1]))
        row_s = both_halves(as_column(mine[1:2]))
        for j in range(count):
            key = block_at(keys_ref, first + j)
            t, s = scores(own[...], key[...])
            key_u = factors(first + j)
            symmetric = jnp.exp2(s) * (row_s + key_u[1:2]) - jnp.exp2(t) * (row_t + key_u[0:1])
            keep = keep_of(j)
            if keep is not None:
                symmetric = jnp.where(keep, symmetric, 0.0)
            sym[:, j * BLOCK : (j + 1) * BLOCK] = symmetric.astype(jnp.bfloat16)
        span = pl.ds(pl.multiple_of(first * BLOCK, BLOCK), count * BLOCK)
        return dot(sym[:, : count * BLOCK], keys_ref[span, WIDE:], NN)

    @pl.when(jnp.logical_and(calm, has_long))
    def _():
        first = docs.long_block

        def keep_of(j):
            if 0 < j < LONG_TILES - 1:
                return None
            return docs.in_longest(across((first + j) * BLOCK))

        total = tiles(first, LONG_TILES, keep_of)
        acc[...] = jnp.where(docs.in_longest(down(own_block * BLOCK)), total, 0.0)

    @pl.when(jnp.logical_and(calm, has_short))
    def _():
        first = short_block
        row_docs = docs.of(down(own_block * BLOCK))

        def keep_of(j):
            return row_docs == docs.of(across((first + j) * BLOCK))

        total = tiles(first, SHORT_TILES, keep_of)
        acc[...] = jnp.where(docs.in_longest(down(own_block * BLOCK)), acc[...], total)

    @pl.when(jnp.logical_not(calm))
    def _():
        for i in range(2):
            row_u[i] = as_column(stats_ref[own_block, i : i + 1] * LOG2E)
        row_u[2] = as_column(stats_ref[own_block, 3:4])
        row_docs = docs.of(down(own_block * BLOCK))
        first = low_block

        @pl.loop(0, all_blocks)
        def _(j):
            key = block_at(keys_ref, first + j)
            t, s = scores(own[...], key[...])
            keep = row_docs == docs.of(across((first + j) * BLOCK))
            key_lse = stats_ref[first + j, 0:2] * LOG2E

            def prob(score, lse):
                return jnp.exp2(jnp.where(keep, score - lse, NEG_FILL))

            pull = both_halves(row_u[2]) * (prob(s, both_halves(row_u[1])) - prob(t, both_halves(row_u[0])))
            pull_t = stats_ref[first + j, 3:4] * (prob(s, key_lse[1:2]) - prob(t, key_lse[0:1]))
            acc[...] += dot((pull + pull_t).astype(jnp.bfloat16), key[:, WIDE:], NN)

    out_ref[...] = (acc[...] * STUDENT_SCALE).astype(out_ref.dtype)


VMEM = pl.BlockSpec(memory_space=pltpu.VMEM)
SMEM = pl.BlockSpec(memory_space=pltpu.SMEM)
ANY = pl.BlockSpec(memory_space=pl.ANY)


def run_early(lengths, blocks, pieces):
    return pl.pallas_call(
        early_kernel,
        out_shape=(
            jax.ShapeDtypeStruct((4, 8, BLOCK), jnp.float32),
            jax.ShapeDtypeStruct((8 * BLOCK, WIDE + NARROW), jnp.bfloat16),
        ),
        in_specs=[SMEM, SMEM] + [VMEM] * 8,
        out_specs=(VMEM, VMEM),
        scratch_shapes=[pltpu.VMEM((8, BLOCK), jnp.float32)],
        compiler_params=pltpu.CompilerParams(vmem_limit_bytes=16 * MIB),
        cost_estimate=pl.CostEstimate(flops=3 * 10**9, bytes_accessed=7 * MIB, transcendentals=0),
        name="early",
    )(lengths, blocks, *pieces)


def run_stats(lengths, blocks, part, half, core, far):
    return pl.pallas_call(
        stats_kernel,
        out_shape=(
            jax.ShapeDtypeStruct((4, 8, BLOCK), jnp.float32),
            jax.ShapeDtypeStruct((4, BLOCK), jnp.float32),
            jax.ShapeDtypeStruct((16 * BLOCK, WIDE + NARROW), jnp.bfloat16),
        ),
        in_specs=[SMEM, SMEM, VMEM, VMEM, ANY, ANY],
        out_specs=(VMEM, VMEM, VMEM),
        scratch_shapes=[pltpu.VMEM((8, BLOCK), jnp.float32)] * 3 + [pltpu.SemaphoreType.DMA((8,))],
        compiler_params=pltpu.CompilerParams(vmem_limit_bytes=20 * MIB),
        cost_estimate=pl.CostEstimate(flops=3 * 10**9, bytes_accessed=7 * MIB, transcendentals=0),
        name="stats",
    )(lengths, blocks, part, half, core, far)


def run_grad(rb, lengths, blocks, stats, keys):
    return pl.pallas_call(
        functools.partial(grad_kernel, rb),
        out_shape=jax.ShapeDtypeStruct((BLOCK, NARROW), jnp.bfloat16),
        in_specs=[SMEM, SMEM, VMEM, VMEM],
        out_specs=VMEM,
        scratch_shapes=[
            pltpu.VMEM((3, BLOCK, 128), jnp.float32),
            pltpu.VMEM((BLOCK, NARROW), jnp.float32),
            pltpu.VMEM((BLOCK, LONG_TILES * BLOCK), jnp.bfloat16),
        ],
        compiler_params=pltpu.CompilerParams(vmem_limit_bytes=16 * MIB),
        cost_estimate=pl.CostEstimate(flops=2 * 10**9, bytes_accessed=7 * MIB, transcendentals=0),
        name="grad",
    )(lengths, blocks, stats, keys)


def after(value, *others):
    return lax.optimization_barrier((value,) + others)[0]


def in_thirds(row):
    high = lax.reduce_precision(row, 8, 7)
    middle = lax.reduce_precision(row - high, 8, 7)
    return [part.astype(jnp.bfloat16) for part in (high, middle, row - high - middle)]


def local(teacher, student, weights, lengths):
    seq = lax.axis_index("seq")
    z, x = seq // 2, seq % 2
    head = lax.axis_index("head")
    c = head % 2
    source = (z // 2) * 2 + c

    items = [ROUNDS[PLANES.index(p)] if p in PLANES else (0, 1, 2, 3) for p in range(8)]
    quarters = [lookup([items[p][k] for p in range(8)], z) for k in range(4)]
    mine = 2 * c + x
    blocks = jnp.stack([q * 4 + mine for q in quarters])

    w_tail = jnp.concatenate(in_thirds(weights.reshape(1, BLOCK)), axis=1)
    w_tail = jnp.pad(w_tail, ((0, 15), (0, 0)))

    def message(k):
        sent = [relation_sent(k, q, core) or 0 for q in range(4) for core in range(2)]
        r = lookup(sent, source)
        vectors = [lax.dynamic_index_in_dim(v, r, 0, False) for v in (teacher, student)]
        return jnp.concatenate([jnp.concatenate(vectors, axis=1), w_tail], axis=0)

    own = [permute(message(k), out_pairs(k)) for k in range(4)]
    mine_only = [v[:BLOCK] for v in own]
    side = [permute(v, swap_pairs(1, 0)) for v in mine_only]
    core = permute(after(jnp.concatenate(mine_only, axis=0), side[1]), swap_pairs(0, 1))
    far = permute(jnp.concatenate(side, axis=0), swap_pairs(0, 1))
    part, half = run_early(lengths, blocks, own + side)
    stats, loss, keys = run_stats(lengths, blocks, part, half, core, far)

    both = jnp.stack([stats, permute(stats, swap_pairs(1, 0))])
    four = [both, permute(both, swap_pairs(0, 1))]
    all_stats = jnp.zeros((16, 8, BLOCK), jnp.float32)
    for flip in range(4):
        for k in range(4):
            where = quarters[k] * 4 + (mine ^ flip)
            all_stats = lax.dynamic_update_slice(
                all_stats, four[flip // 2][flip % 2, k : k + 1], (where, 0, 0)
            )
    grads = []
    for step, dh in enumerate((2, 4, 8)):
        loss = after(loss, all_stats if step == 0 else grads[step - 1])
        came = permute(loss, [(place(z, x, g, c), place(z, x, g, c) ^ dh) for z, x, g, c in DEVICES])
        grads.append(run_grad(step, lengths, blocks, all_stats, keys))
        loss = loss + came
        blocks = after(blocks, loss)
    grads.append(run_grad(3, lengths, blocks, all_stats, keys))

    back = []
    for k in range(4):
        tail = jnp.concatenate(in_thirds(lax.dynamic_slice_in_dim(loss, quarters[k], 1, 0)), axis=0)
        tail = jnp.pad(tail, ((0, 13), (0, 0)))
        back.append(permute(jnp.concatenate([grads[k], tail], axis=0), back_pairs(k)))
    total = sum(v[BLOCK : BLOCK + 3].astype(jnp.float32) for v in back)
    total = jnp.sum(total, axis=0, keepdims=True)
    total = total + permute(
        total, [(place(z, x, g, c), place(z, x, g, c) ^ 1) for z, x, g, c in DEVICES]
    )
    row_loss = total.reshape(BLOCK)

    back = jnp.stack([v[:BLOCK] for v in back])
    came = []
    for r in range(3):
        table = [ROUNDS[core * 3 + r].index(q) for q in range(4) for core in range(2)]
        came.append(lax.dynamic_index_in_dim(back, lookup(table, source), 0, False))
    return (row_loss, jnp.stack(came).astype(jnp.float32))


def solution(mesh):
    return jax.shard_map(
        local,
        mesh=mesh,
        in_specs=(P(None, "seq", "head"), P(None, "seq", "head"), P("seq"), P()),
        out_specs=(P("seq"), P(None, "seq", "head")),
        check_vma=False,
    )
```
